32 devices in a mesh: img: 16 (over z, y, core), ch: 2 (over x).
Axes of the slice: x: 2, y: 2, z: 4, core: 2. Of those that a mesh axis runs over, the one named last changes fastest.
Arguments:
- activations: bfloat16 [192, 56, 2048], P('img', None, 'ch'), may hold values from -6 to 6
- filters: bfloat16 [3, 3, 2048, 4096], P(None, None, 'img', 'ch'), may hold values from -0.046875 to 0.046875
- channel_bias: float32 [4096], P('ch'), may hold values from -3 to 3
Outputs:
- convolved: bfloat16 [192, 56, 4096], P('img', None, 'ch')
The draws below stay inside these ranges and needn't reach their ends.
All inputs are finite; a program needn't handle non-finite values.
Results may differ from the reference program's by a relative error of at most 0.001.
Values may be sent and summed in bfloat16 or wider, within the bound.
No kernel may reach another device: no remote copies, remote signals or barrier semaphores. Data moves between devices by JAX's collectives and lax.ppermute only.
A program may use at most 192 MiB of HBM per device.

```python
import jax
import jax.numpy as jnp

CIN = 2048
COUT = 4096
SIDE = 56
ROWS = 192


def block_levels(own_key, shape, cuts, smallest, largest):
    factor_of = 1.0
    for position, blocks in cuts:
        steps = jax.random.uniform(jax.random.fold_in(jax.random.fold_in(own_key, 6), position), (blocks,), jnp.float32, smallest / len(cuts), largest / len(cuts))
        factor_of = factor_of * jnp.repeat(jnp.exp(steps), shape[position] // blocks).reshape((-1,) + (1,) * (len(shape) - 1 - position))
    return factor_of


def normal_values(rng, dims, deviation, reach, pieces=(), kind=jnp.bfloat16):
    result = deviation * jax.random.normal(rng, dims, jnp.float32)
    if pieces:
        result = result * block_levels(rng, dims, pieces, -0.22, 0.18)
    return jnp.clip(result, -reach, reach).astype(kind)


def setup_inputs(seed: int = 0) -> dict:
    splits = jax.random.split(jax.random.key(seed), 4)
    activations = normal_values(splits[0], (ROWS, SIDE, CIN), 1.0, 6.0, ((0, 16), (2, 2)))
    filters = normal_values(splits[1], (3, 3, CIN, COUT), (9 * CIN) ** -0.5, 0.046875, ((2, 16), (3, 2)))
    channel_bias = normal_values(splits[2], (COUT,), 0.5, 3.0, ((0, 2),), jnp.float32)
    return {"activations": activations, "filters": filters, "channel_bias": channel_bias}


def reference(activations, filters, channel_bias):
    row_count = activations.shape[0]
    global_rows = jnp.arange(row_count, dtype=jnp.int32)
    above_mask = (global_rows % SIDE != 0).astype(activations.dtype)
    below_mask = ((global_rows + 1) % SIDE != 0).astype(activations.dtype)
    padded = jnp.pad(activations, ((1, 1), (1, 1), (0, 0)))
    shifted = [padded[:row_count] * above_mask[:, None, None], padded[1:row_count + 1], padded[2:] * below_mask[:, None, None]]
    accumulated = jnp.zeros((row_count * SIDE, filters.shape[3]), jnp.float32)
    for vertical in range(3):
        for horizontal in range(3):
            operand = shifted[vertical][:, horizontal:horizontal + SIDE, :].reshape(row_count * SIDE, -1)
            accumulated = accumulated + jnp.dot(operand, filters[vertical, horizontal], preferred_element_type=jnp.float32)
    output = accumulated + channel_bias[None, :].astype(jnp.float32)
    return output.astype(jnp.bfloat16).reshape(row_count, SIDE, -1)
```

```python
import functools

import jax
import jax.numpy as jnp
from jax import lax
from jax.experimental import pallas as pl
from jax.experimental.pallas import tpu as pltpu
from jax.sharding import PartitionSpec as P

SIDE = 56
GROUP = 8
TILE = 8


def swap(array, axis, bit):
    size = lax.axis_size(axis)
    return lax.ppermute(array, axis, [(i, i ^ bit) for i in range(size)])


def tap_kernel(shift, parts, last, scalars, image, *refs):
    weights, (acc_in, bias, out) = refs[:parts], refs[parts:]
    tile = pl.program_id(0)
    first_row, group = scalars[0], scalars[1]
    blocks, _, width, depth = image.shape
    per_part = blocks // parts
    rows = TILE
    row = first_row + tile * rows + lax.broadcasted_iota(jnp.int32, (rows, 1, 1), 0)
    total = None
    for vertical in range(3):
        part_sum = None
        for part in range(parts):
            for inner in range(per_part):
                block = (group ^ part) * per_part + inner
                operand = image[block, pl.ds(vertical, rows)].reshape(rows * width, depth)
                term = jnp.dot(
                    operand,
                    weights[part][vertical, pl.ds(inner * depth, depth), :],
                    preferred_element_type=jnp.float32,
                )
                part_sum = term if part_sum is None else part_sum + term
        part_sum = part_sum.reshape(rows, width, -1)
        if vertical == 0:
            part_sum = jnp.where(row % SIDE != 0, part_sum, 0.0)
        if vertical == 2:
            part_sum = jnp.where((row + 1) % SIDE != 0, part_sum, 0.0)
        total = part_sum if total is None else total + part_sum
    if shift:
        total = pltpu.roll(total, shift % width, 1)
    if acc_in is not None:
        total = total + acc_in[...]
    if last:
        total = total + bias[...].reshape(1, 1, -1)
    out[...] = total.astype(out.dtype)


def tap_call(shift, scalars, image, weights, acc, bias):
    blocks, padded_rows, width, depth = image.shape
    out_width = weights[0].shape[2]
    row_count = padded_rows - 2
    last = acc is not None and bias is not None
    parts = len(weights)

    def body(scalars_ref, image_ref, *refs):
        refs = list(refs)
        weight_refs, refs = refs[:parts], refs[parts:]
        acc_ref = refs.pop(0) if acc is not None else None
        bias_ref = refs.pop(0) if bias is not None else None
        tap_kernel(shift, parts, last, scalars_ref, image_ref, *weight_refs, acc_ref, bias_ref, refs[0])

    tile_spec = pl.BlockSpec((TILE, width, out_width), lambda t, s: (t, 0, 0))
    in_specs = [
        pl.BlockSpec(
            (pl.Element(blocks), pl.Element(TILE + 2), pl.Element(width), pl.Element(depth)),
            lambda t, s: (0, t * TILE, 0, 0),
        )
    ]
    operands = [image, *weights]
    for weight in weights:
        in_specs.append(pl.BlockSpec(weight.shape, lambda t, s: (0, 0, 0)))
    if acc is not None:
        in_specs.append(tile_spec)
        operands.append(acc)
    if bias is not None:
        in_specs.append(pl.BlockSpec((1, out_width), lambda t, s: (0, 0)))
        operands.append(bias)
    macs = row_count * width * 3 * blocks * depth * out_width
    return pl.pallas_call(
        body,
        grid_spec=pltpu.PrefetchScalarGridSpec(
            num_scalar_prefetch=1,
            grid=(row_count // TILE,),
            in_specs=in_specs,
            out_specs=tile_spec,
        ),
        out_shape=jax.ShapeDtypeStruct(
            (row_count, width, out_width), jnp.bfloat16 if last else jnp.float32
        ),
        compiler_params=pltpu.CompilerParams(vmem_limit_bytes=40 * 1024 * 1024),
        cost_estimate=pl.CostEstimate(
            flops=2 * macs, bytes_accessed=2 * image.size, transcendentals=0
        ),
    )(scalars, *operands)


def local(activations, filters, channel_bias):
    rows, side, depth = activations.shape
    out_local = filters.shape[3]
    size, chans = lax.axis_size("img"), lax.axis_size("ch")
    me, mine = lax.axis_index("img"), lax.axis_index("ch")
    parts = size // GROUP
    group, rank = me // GROUP, me % GROUP
    members = [[g * GROUP + r for r in range(GROUP)] for g in range(parts)]
    split = out_local // GROUP

    weights = []
    for horizontal in range(3):
        own = lax.all_to_all(
            filters[:, horizontal], "img", 2, 1, axis_index_groups=members, tiled=True
        )
        weights.append([own] + [swap(own, "img", GROUP * j) for j in range(1, parts)])

    edges = [(g * GROUP - 1, g * GROUP) for g in range(1, parts)]
    above = lax.ppermute(activations[-1:], "img", edges)
    below = lax.ppermute(activations[:1], "img", [(j, i) for i, j in edges])
    halo = jnp.where(rank == 0, above, below)
    piece = jnp.concatenate([activations, halo], axis=0)
    slots = {(0, 0): piece}
    slots[0, 4] = swap(piece, "img", 4)
    slots[0, 2] = swap(piece, "img", 2)
    slots[0, 6] = swap(slots[0, 4], "img", 2)
    for j in range(1, chans):
        for r in (0, 4, 2, 6):
            slots[j, r] = swap(slots[0, r], "ch", j)
    for (j, r), value in list(slots.items()):
        slots[j, r + 1] = swap(value, "img", 1)
    width = -(-side // 16) * 16
    image = jnp.zeros((chans, GROUP * rows + 2, width, depth), activations.dtype)
    for (j, r), value in slots.items():
        image = lax.dynamic_update_slice(
            image, value[None, :rows], (mine ^ j, (rank ^ r) * rows + 1, 0, 0)
        )
    for j in range(chans):
        stack = jnp.stack([slots[j, r][rows:] for r in range(GROUP)])
        top = lax.dynamic_index_in_dim(stack, rank, 0)
        bottom = lax.dynamic_index_in_dim(stack, rank ^ (GROUP - 1), 0)
        image = lax.dynamic_update_slice(image, top, (mine ^ j, 0, 0, 0))
        image = lax.dynamic_update_slice(image, bottom, (mine ^ j, GROUP * rows + 1, 0, 0))

    scalars = jnp.stack([group * GROUP * rows, group]).astype(jnp.int32)
    bias = lax.dynamic_slice_in_dim(channel_bias, rank * split, split)[None]
    acc = tap_call(1, scalars, image, weights[0], None, None)
    acc = tap_call(0, scalars, image, weights[1], acc, None)
    out = tap_call(-1, scalars, image, weights[2], acc, bias)[:, :side]
    return lax.all_to_all(out, "img", 0, 2, axis_index_groups=members, tiled=True)


def solution(mesh):
    placed = (P("img", None, "ch"), P(None, None, "img", "ch"), P("ch"))
    return jax.shard_map(
        local, mesh=mesh, in_specs=placed, out_specs=P("img", None, "ch"), check_vma=False
    )
```

```python
import jax
import jax.numpy as jnp
from jax import lax
from jax.experimental import pallas as pl
from jax.experimental.pallas import tpu as pltpu
from jax.sharding import PartitionSpec as P

SIDE = 56
GROUP = 8
TILE = 8
CHUNKS = 4


def swap(array, axis, bit):
    size = lax.axis_size(axis)
    return lax.ppermute(array, axis, [(i, i ^ bit) for i in range(size)])


def after(array, *others):
    return lax.optimization_barrier((array, *others))[0]


def conv_call(taps, pieces, scalars, image, acc=None, bias=None):
    blocks, padded_rows, width, depth = image.shape
    shard, out_width = pieces[0][2].shape[2:]
    row_count = padded_rows - 2
    offsets = sorted({offset for offset, _, _ in pieces})
    per_group = GROUP * shard // depth
    first, count = min(taps), len(taps)
    final = bias is not None

    def body(scalars_ref, *refs):
        refs = list(refs)
        images = {offset: refs.pop(0) for offset in offsets}
        weights = [refs.pop(0) for _ in pieces]
        acc_ref = refs.pop(0) if acc is not None else None
        bias_ref = refs.pop(0) if final else None
        out = refs.pop(0)
        row = (
            scalars_ref[0]
            + pl.program_id(0) * TILE
            + lax.broadcasted_iota(jnp.int32, (TILE, 1, 1), 0)
        )
        total = None
        for horizontal in range(3):
            across = None
            for index, vertical in enumerate(taps):
                value = None
                for (offset, start, array), weight in zip(pieces, weights):
                    lanes = array.shape[0] * shard
                    flat = weight[:, 3 * index + horizontal].reshape(lanes, out_width)
                    low = start * shard
                    while low < start * shard + lanes:
                        inner, lane = divmod(low, depth)
                        size = min(depth - lane, start * shard + lanes - low)
                        operand = images[offset][
                            inner, pl.ds(vertical - first, TILE), :, pl.ds(lane, size)
                        ].reshape(TILE * width, size)
                        at = low - start * shard
                        term = jnp.dot(
                            operand, flat[at : at + size], preferred_element_type=jnp.float32
                        )
                        value = term if value is None else value + term
                        low += size
                value = value.reshape(TILE, width, out_width)
                if vertical == 0:
                    value = jnp.where(row % SIDE != 0, value, 0.0)
                if vertical == 2:
                    value = jnp.where((row + 1) % SIDE != 0, value, 0.0)
                across = value if across is None else across + value
            if horizontal != 1:
                across = pltpu.roll(across, (1 - horizontal) % width, 1)
            total = across if total is None else total + across
        if acc_ref is not None:
            total = total + acc_ref[...]
        if final:
            total = (total + bias_ref[...].reshape(1, 1, -1))[:, : out.shape[1]]
        out[...] = total.astype(out.dtype)

    def image_spec(offset):
        return pl.BlockSpec(
            (
                pl.Element(per_group),
                pl.Element(TILE + count - 1),
                pl.Element(width),
                pl.Element(depth),
            ),
            lambda t, s: ((s[1] ^ offset) * per_group, t * TILE + first, 0, 0),
        )

    out_cols = SIDE if final else width
    in_specs = [image_spec(offset) for offset in offsets]
    operands = [image] * len(offsets)
    for _, _, array in pieces:
        in_specs.append(pl.BlockSpec(array.shape, lambda t, s: (0, 0, 0, 0)))
        operands.append(array)
    if acc is not None:
        in_specs.append(pl.BlockSpec((TILE, width, out_width), lambda t, s: (t, 0, 0)))
        operands.append(acc)
    if final:
        in_specs.append(pl.BlockSpec((1, out_width), lambda t, s: (0, 0)))
        operands.append(bias)
    channels = sum(array.shape[0] for _, _, array in pieces) * shard
    return pl.pallas_call(
        body,
        grid_spec=pltpu.PrefetchScalarGridSpec(
            num_scalar_prefetch=1,
            grid=(row_count // TILE,),
            in_specs=in_specs,
            out_specs=pl.BlockSpec((TILE, out_cols, out_width), lambda t, s: (t, 0, 0)),
        ),
        out_shape=jax.ShapeDtypeStruct(
            (row_count, out_cols, out_width), jnp.bfloat16 if final else jnp.float32
        ),
        compiler_params=pltpu.CompilerParams(vmem_limit_bytes=40 * 1024 * 1024),
        cost_estimate=pl.CostEstimate(
            flops=2 * row_count * width * 3 * count * channels * out_width,
            bytes_accessed=2 * image.size,
            transcendentals=0,
        ),
    )(scalars, *operands)


def local(activations, filters, channel_bias):
    rows, side, depth = activations.shape
    shard, out_local = filters.shape[2:]
    size, chans = lax.axis_size("img"), lax.axis_size("ch")
    me, mine = lax.axis_index("img"), lax.axis_index("ch")
    parts = size // GROUP
    group, rank = me // GROUP, me % GROUP
    members = [[g * GROUP + r for r in range(GROUP)] for g in range(parts)]
    split = out_local // GROUP

    def share(taps):
        return lax.all_to_all(taps, "img", 0, 0, axis_index_groups=members, tiled=True)

    def by_member(array):
        return jnp.moveaxis(array.reshape(*array.shape[:-1], GROUP, split), -2, 0)

    raw = [by_member(filters[0, b]) for b in range(3)]
    chain = []
    others = {}
    for b in range(3):
        for j in range(1, parts):
            sent = raw[b] if len(chain) < 2 else after(raw[b], chain[-2])
            others[j, b] = swap(sent, "img", GROUP * j)
            chain.append(others[j, b])
    lower = share(by_member(filters[1:].reshape(6, shard, out_local)))
    step = GROUP // CHUNKS
    received = []
    for chunk in range(CHUNKS):
        for j in range(1, parts):
            sent = after(lower[chunk * step : (chunk + 1) * step], chain[-2])
            received.append((j, chunk * step, swap(sent, "img", GROUP * j)))
            chain.append(received[-1][2])
    stacked = [jnp.stack(raw, 1)] + [
        jnp.stack([others[j, b] for b in range(3)], 1) for j in range(1, parts)
    ]
    upper = [(j, 0, share(stacked[j])) for j in range(parts)]

    ups = [(i, i + 1) for i in range(size - 1)]
    above = lax.ppermute(activations[-1:], "img", ups)
    below = lax.ppermute(activations[:1], "img", [(j, i) for i, j in ups])
    late = rank >= GROUP // 2
    piece = jnp.where(
        late,
        jnp.concatenate([activations, below], axis=0),
        jnp.concatenate([above, activations], axis=0),
    )
    slots = {(0, 0): piece}
    slots[0, 4] = swap(piece, "img", 4)
    slots[0, 2] = swap(piece, "img", 2)
    slots[0, 6] = swap(slots[0, 4], "img", 2)
    sent = None
    for r in (0, 4, 2, 6):
        for j in range(1, chans):
            slots[j, r] = swap(slots[0, r] if sent is None else after(slots[0, r], sent), "ch", j)
        sent = slots[1, r]
    for (j, r), value in list(slots.items()):
        slots[j, r + 1] = swap(value, "img", 1)
    width = -(-side // 16) * 16
    image = jnp.zeros((chans, GROUP * rows + 2, width, depth), activations.dtype)
    for (j, r), value in slots.items():
        owner = rank ^ r
        start = owner * rows + (owner >= GROUP // 2).astype(jnp.int32)
        image = lax.dynamic_update_slice(image, value[None], (mine ^ j, start, 0, 0))

    scalars = jnp.stack([group * GROUP * rows, group]).astype(jnp.int32)
    bias = lax.dynamic_slice_in_dim(channel_bias, rank * split, split)[None]
    most = (CHUNKS - 1) * (parts - 1)
    acc = conv_call((1, 2), [(0, 0, lower)], scalars, image)
    acc = conv_call((0,), upper, scalars, image, acc)
    acc = conv_call((1, 2), received[:most], scalars, image, acc)
    out = conv_call((1, 2), received[most:], scalars, image, acc, bias)
    out = share(out).reshape(GROUP, rows, side, split)
    return jnp.moveaxis(out, 0, 2).reshape(rows, side, out_local)


def solution(mesh):
    placed = (P("img", None, "ch"), P(None, None, "img", "ch"), P("ch"))
    return jax.shard_map(
        local, mesh=mesh, in_specs=placed, out_specs=P("img", None, "ch"), check_vma=False
    )
```

```python
import jax
import jax.numpy as jnp
from jax import lax
from jax.experimental import pallas as pl
from jax.experimental.pallas import tpu as pltpu
from jax.sharding import PartitionSpec as P

SIDE = 56
GROUP = 8
TILE = 8
CHUNKS = 4


def swap(array, axis, bit):
    size = lax.axis_size(axis)
    return lax.ppermute(array, axis, [(i, i ^ bit) for i in range(size)])


def after(array, *others):
    return lax.optimization_barrier((array, *others))[0]


def conv_call(taps, pieces, scalars, image, acc=None, bias=None):
    blocks, padded_rows, width, depth = image.shape
    shard, out_width = pieces[0][2].shape[2:]
    row_count = padded_rows - 3
    offsets = sorted({offset for offset, _, _ in pieces})
    per_group = GROUP * shard // depth
    final = bias is not None
    assert row_count % TILE == 0 and SIDE % TILE == 0

    windows = {}
    for offset in offsets:
        low = min(start for o, start, _ in pieces if o == offset) * shard
        high = max(start + a.shape[0] for o, start, a in pieces if o == offset) * shard
        if low // depth == (high - 1) // depth:
            windows[offset] = (1, low // depth, high - low, low % depth)
        else:
            windows[offset] = (per_group, 0, depth, 0)

    def body(scalars_ref, *refs):
        refs = list(refs)
        images = {}
        for offset in offsets:
            images[offset] = refs.pop(0), *(refs.pop(0) for v in taps if v != 1)
        weights = [refs.pop(0) for _ in pieces]
        acc_ref = refs.pop(0) if acc is not None else None
        bias_ref = refs.pop(0) if final else None
        out = refs.pop(0)

        operands, columns = [], []
        for (offset, start, array), weight in zip(pieces, weights):
            count, first_block, size, first_lane = windows[offset]
            main, *outer = images[offset]
            at, lanes = 0, array.shape[0] * shard
            while at < lanes:
                inner, lane = divmod(start * shard + at, depth)
                inner, lane = inner - first_block, lane - first_lane
                length = min(size - lane, lanes - at)
                window = pl.ds(lane, length)
                edges = list(outer)
                for index, vertical in enumerate(taps):
                    rows = main[inner, :, :, window]
                    if vertical == 0:
                        rows = jnp.concatenate(
                            [edges.pop(0)[inner, :, :, window], rows[:-1]], axis=0
                        )
                    if vertical == 2:
                        rows = jnp.concatenate(
                            [rows[1:], edges.pop(0)[inner, :, :, window]], axis=0
                        )
                    operands.append(rows.reshape(TILE * width, length))
                    members = pl.ds(at // shard, length // shard)
                    columns.append(
                        [
                            weight[members, 3 * index + b].reshape(length, out_width)
                            for b in range(3)
                        ]
                    )
                at += length
        operand = jnp.concatenate(operands, axis=1)
        total = None
        for horizontal in range(3):
            value = jnp.dot(
                operand,
                jnp.concatenate([c[horizontal] for c in columns], axis=0),
                preferred_element_type=jnp.float32,
            ).reshape(TILE, width, out_width)
            if horizontal != 1:
                value = pltpu.roll(value, (1 - horizontal) % width, 1)
            total = value if total is None else total + value
        if acc_ref is not None:
            total = total + acc_ref[...]
        if final:
            total = (total + bias_ref[...].reshape(1, 1, -1))[:, : out.shape[1]]
        out[...] = total.astype(out.dtype)

    def image_spec(offset, vertical):
        count, first_block, size, first_lane = windows[offset]
        rows = TILE if vertical == 1 else 1

        def place(t, s):
            row = t * TILE + 1
            if vertical == 0:
                row = jnp.where((s[0] + t * TILE) % SIDE == 0, row_count + 2, row - 1)
            if vertical == 2:
                row = jnp.where((s[0] + (t + 1) * TILE) % SIDE == 0, row_count + 2, row + TILE)
            return ((s[1] ^ offset) * per_group + first_block, row, 0, first_lane)

        return pl.BlockSpec(tuple(pl.Element(n) for n in (count, rows, width, size)), place)

    out_cols = SIDE if final else width
    in_specs, operands = [], []
    for offset in offsets:
        for vertical in [1] + [v for v in taps if v != 1]:
            in_specs.append(image_spec(offset, vertical))
            operands.append(image)
    for _, _, array in pieces:
        in_specs.append(pl.BlockSpec(array.shape, lambda t, s: (0, 0, 0, 0)))
        operands.append(array)
    if acc is not None:
        in_specs.append(pl.BlockSpec((TILE, width, out_width), lambda t, s: (t, 0, 0)))
        operands.append(acc)
    if final:
        in_specs.append(pl.BlockSpec((1, out_width), lambda t, s: (0, 0)))
        operands.append(bias)
    return pl.pallas_call(
        body,
        grid_spec=pltpu.PrefetchScalarGridSpec(
            num_scalar_prefetch=1,
            grid=(row_count // TILE,),
            in_specs=in_specs,
            out_specs=pl.BlockSpec((TILE, out_cols, out_width), lambda t, s: (t, 0, 0)),
        ),
        out_shape=jax.ShapeDtypeStruct(
            (row_count, out_cols, out_width), jnp.bfloat16 if final else jnp.float32
        ),
        compiler_params=pltpu.CompilerParams(vmem_limit_bytes=40 * 1024 * 1024),
        cost_estimate=pl.CostEstimate(flops=1024, bytes_accessed=1024, transcendentals=0),
    )(scalars, *operands)


def by_member(filters, first, count):
    _, across, shard, out_local = filters.shape
    split = out_local // GROUP
    if split % 128:
        taps = filters[first : first + count].reshape(count * across, shard, out_local)
        return jnp.stack([taps[..., r * split : (r + 1) * split] for r in range(GROUP)])

    def body(taps, out):
        out[...] = taps[...].reshape(out.shape)

    return pl.pallas_call(
        body,
        grid=(GROUP, count),
        in_specs=[
            pl.BlockSpec((1, across, shard, split), lambda r, v: (first + v, 0, 0, r))
        ],
        out_specs=pl.BlockSpec((1, across, shard, split), lambda r, v: (r, v, 0, 0)),
        out_shape=jax.ShapeDtypeStruct((GROUP, count * across, shard, split), filters.dtype),
    )(filters)


def local(activations, filters, channel_bias):
    rows, side, depth = activations.shape
    shard, out_local = filters.shape[2:]
    size, chans = lax.axis_size("img"), lax.axis_size("ch")
    me, mine = lax.axis_index("img"), lax.axis_index("ch")
    parts = size // GROUP
    group, rank = me // GROUP, me % GROUP
    members = [[g * GROUP + r for r in range(GROUP)] for g in range(parts)]
    split = out_local // GROUP

    def share(taps):
        return lax.all_to_all(taps, "img", 0, 0, axis_index_groups=members, tiled=True)

    raw = [swap(filters[0], "img", GROUP * j) for j in range(1, parts)]

    ups = [(i, i + 1) for i in range(size - 1)]
    above = lax.ppermute(activations[-1:], "img", ups)
    below = lax.ppermute(activations[:1], "img", [(j, i) for i, j in ups])
    piece = jnp.where(
        rank >= GROUP // 2,
        jnp.concatenate([activations, below], axis=0),
        jnp.concatenate([above, activations], axis=0),
    )
    slots = {(0, 0): piece}

    def cross(r, *others):
        sent = after(slots[0, r], *others) if others else slots[0, r]
        for j in range(1, chans):
            slots[j, r] = swap(sent, "ch", j)

    cross(0)
    slots[0, 4] = swap(piece, "img", 4)
    slots[0, 2] = swap(piece, "img", 2)
    cross(4, slots[1, 0])
    cross(2, slots[1, 4])

    lower = share(after(by_member(filters, 1, 2), slots[0, 4], slots[0, 2]))
    step = GROUP // CHUNKS
    received = []

    def exchange(chunk, *others):
        sent = after(lower[chunk * step : (chunk + 1) * step], *others)
        for j in range(1, parts):
            received.append((j, chunk * step, swap(sent, "img", GROUP * j)))

    exchange(0, *raw)
    exchange(1, *raw)
    slots[0, 6] = swap(after(slots[0, 4], lower), "img", 2)
    exchange(2, received[0][2])
    cross(6, slots[1, 2])
    upper = [
        (j, 0, share(by_member(after(taps, received[0][2]), 0, 1)))
        for j, taps in enumerate([filters] + [array[None] for array in raw])
    ]
    exchange(3, received[parts - 1][2])

    for (j, r), value in list(slots.items()):
        slots[j, r + 1] = swap(value, "img", 1)
    width = -(-side // 16) * 16
    image = jnp.zeros((chans, GROUP * rows + 3, width, depth), activations.dtype)
    for (j, r), value in slots.items():
        owner = rank ^ r
        start = owner * rows + (owner >= GROUP // 2).astype(jnp.int32)
        image = lax.dynamic_update_slice(image, value[None], (mine ^ j, start, 0, 0))

    scalars = jnp.stack([group * GROUP * rows, group]).astype(jnp.int32)
    bias = lax.dynamic_slice_in_dim(channel_bias, rank * split, split)[None]
    most = (CHUNKS - 1) * (parts - 1)
    acc = conv_call((1, 2), [(0, 0, lower)], scalars, image)
    acc = conv_call((0,), upper, scalars, image, acc)
    acc = conv_call((1, 2), received[:most], scalars, image, acc)
    out = conv_call((1, 2), received[most:], scalars, image, acc, bias)
    out = share(out).reshape(GROUP, rows, side, split)
    return jnp.moveaxis(out, 0, 2).reshape(rows, side, out_local)


def solution(mesh):
    placed = (P("img", None, "ch"), P(None, None, "img", "ch"), P("ch"))
    return jax.shard_map(
        local, mesh=mesh, in_specs=placed, out_specs=P("img", None, "ch"), check_vma=False
    )
```

```python
import jax
import jax.numpy as jnp
from jax import lax
from jax.experimental import pallas as pl
from jax.experimental.pallas import tpu as pltpu
from jax.sharding import PartitionSpec as P

SIDE = 56
GROUP = 8
TILE = 8
CHUNKS = 4


def swap(array, axis, bit):
    size = lax.axis_size(axis)
    return lax.ppermute(array, axis, [(i, i ^ bit) for i in range(size)])


def after(array, *others):
    return lax.optimization_barrier((array, *others))[0]


def conv_call(taps, pieces, scalars, image, acc=None, bias=None):
    blocks, padded_rows, width, depth = image.shape
    shard, out_width = pieces[0][2].shape[-2:]
    row_count = padded_rows - 3
    offsets = list(dict.fromkeys(piece[0] for piece in pieces))
    per_group = GROUP * shard // depth
    final = bias is not None
    assert row_count % TILE == 0 and SIDE % TILE == 0

    windows = {}
    for offset in offsets:
        ranges = [(start, start + block[-4]) for o, start, _, block, _ in pieces if o == offset]
        low, high = min(a for a, _ in ranges) * shard, max(b for _, b in ranges) * shard
        if low // depth == (high - 1) // depth:
            windows[offset] = (1, low // depth, high - low, low % depth)
        else:
            windows[offset] = (per_group, 0, depth, 0)

    def body(scalars_ref, *refs):
        refs = list(refs)
        images = {}
        for offset in offsets:
            images[offset] = refs.pop(0), *(refs.pop(0) for v in taps if v != 1)
        weights = [refs.pop(0) for _ in pieces]
        acc_ref = refs.pop(0) if acc is not None else None
        bias_ref = refs.pop(0) if final else None
        out = refs.pop(0)

        operands, columns = [], []
        for (offset, start, _, block, _), weight in zip(pieces, weights):
            count, first_block, size, first_lane = windows[offset]
            main, *outer = images[offset]
            at, lanes = 0, block[-4] * shard
            while at < lanes:
                inner, lane = divmod(start * shard + at, depth)
                inner, lane = inner - first_block, lane - first_lane
                length = min(size - lane, lanes - at)
                window = pl.ds(lane, length)
                edges = list(outer)
                for index, vertical in enumerate(taps):
                    rows = main[inner, :, :, window]
                    if vertical == 0:
                        rows = jnp.concatenate(
                            [edges.pop(0)[inner, :, :, window], rows[:-1]], axis=0
                        )
                    if vertical == 2:
                        rows = jnp.concatenate(
                            [rows[1:], edges.pop(0)[inner, :, :, window]], axis=0
                        )
                    operands.append(rows.reshape(TILE * width, length))
                    members = pl.ds(at // shard, length // shard)
                    columns.append(
                        [
                            weight[members, 3 * index + b].reshape(length, out_width)
                            for b in range(3)
                        ]
                    )
                at += length
        operand = jnp.concatenate(operands, axis=1)
        total = None
        for horizontal in range(3):
            value = jnp.dot(
                operand,
                jnp.concatenate([c[horizontal] for c in columns], axis=0),
                preferred_element_type=jnp.float32,
            ).reshape(TILE, width, out_width)
            if horizontal != 1:
                value = pltpu.roll(value, (1 - horizontal) % width, 1)
            total = value if total is None else total + value
        if acc_ref is not None:
            total = total + acc_ref[...]
        if final:
            total = (total + bias_ref[...].reshape(1, 1, -1))[:, : out.shape[1]]
        out[...] = total.astype(out.dtype)

    def image_spec(offset, vertical):
        count, first_block, size, first_lane = windows[offset]
        rows = TILE if vertical == 1 else 1

        def place(t, s):
            row = t * TILE + 1
            if vertical == 0:
                row = jnp.where((s[0] + t * TILE) % SIDE == 0, row_count + 2, row - 1)
            if vertical == 2:
                row = jnp.where((s[0] + (t + 1) * TILE) % SIDE == 0, row_count + 2, row + TILE)
            return (offset(s) * per_group + first_block, row, 0, first_lane)

        return pl.BlockSpec(tuple(pl.Element(n) for n in (count, rows, width, size)), place)

    out_cols = SIDE if final else width
    in_specs, operands = [], []
    for offset in offsets:
        for vertical in [1] + [v for v in taps if v != 1]:
            in_specs.append(image_spec(offset, vertical))
            operands.append(image)
    for _, _, array, block, place in pieces:
        in_specs.append(pl.BlockSpec(block, lambda t, s, place=place: place(s)))
        operands.append(array)
    if acc is not None:
        in_specs.append(pl.BlockSpec((TILE, width, out_width), lambda t, s: (t, 0, 0)))
        operands.append(acc)
    if final:
        in_specs.append(pl.BlockSpec((1, out_width), lambda t, s: (0, 0)))
        operands.append(bias)
    return pl.pallas_call(
        body,
        grid_spec=pltpu.PrefetchScalarGridSpec(
            num_scalar_prefetch=1,
            grid=(row_count // TILE,),
            in_specs=in_specs,
            out_specs=pl.BlockSpec((TILE, out_cols, out_width), lambda t, s: (t, 0, 0)),
        ),
        out_shape=jax.ShapeDtypeStruct(
            (row_count, out_cols, out_width), jnp.bfloat16 if final else jnp.float32
        ),
        compiler_params=pltpu.CompilerParams(vmem_limit_bytes=40 * 1024 * 1024),
        cost_estimate=pl.CostEstimate(flops=1024, bytes_accessed=1024, transcendentals=0),
    )(scalars, *operands)


def by_member(filters, first, count):
    _, across, shard, out_local = filters.shape
    split = out_local // GROUP
    if split % 128:
        taps = filters[first : first + count].reshape(count * across, shard, out_local)
        return jnp.stack([taps[..., r * split : (r + 1) * split] for r in range(GROUP)])

    def body(taps, out):
        out[...] = taps[...].reshape(out.shape)

    return pl.pallas_call(
        body,
        grid=(GROUP, count),
        in_specs=[
            pl.BlockSpec((1, across, shard, split), lambda r, v: (first + v, 0, 0, r))
        ],
        out_specs=pl.BlockSpec((1, across, shard, split), lambda r, v: (r, v, 0, 0)),
        out_shape=jax.ShapeDtypeStruct((GROUP, count * across, shard, split), filters.dtype),
    )(filters)


def local(activations, filters, channel_bias):
    rows, side, depth = activations.shape
    shard, out_local = filters.shape[2:]
    size, chans = lax.axis_size("img"), lax.axis_size("ch")
    me, mine = lax.axis_index("img"), lax.axis_index("ch")
    parts = size // GROUP
    group, rank = me // GROUP, me % GROUP
    members = [[g * GROUP + r for r in range(GROUP)] for g in range(parts)]
    split = out_local // GROUP

    def share(taps):
        return lax.all_to_all(taps, "img", 0, 0, axis_index_groups=members, tiled=True)

    def exchange(array):
        groups = [[g * GROUP + r for g in range(parts)] for r in range(GROUP)]
        return lax.all_gather(array, "img", axis_index_groups=groups)

    raw = exchange(filters[0])

    ups = [(i, i + 1) for i in range(size - 1)]
    above = lax.ppermute(activations[-1:], "img", ups)
    below = lax.ppermute(activations[:1], "img", [(j, i) for i, j in ups])
    piece = jnp.where(
        rank >= GROUP // 2,
        jnp.concatenate([activations, below], axis=0),
        jnp.concatenate([above, activations], axis=0),
    )
    slots = {(0, 0): piece}

    def cross(r, *others):
        sent = after(slots[0, r], *others) if others else slots[0, r]
        for j in range(1, chans):
            slots[j, r] = swap(sent, "ch", j)

    cross(0)
    slots[0, 4] = swap(piece, "img", 4)
    slots[0, 2] = swap(piece, "img", 2)
    cross(4, slots[1, 0])
    cross(2, slots[1, 4])

    lower = share(after(by_member(filters, 1, 2), slots[0, 4], slots[0, 2], slots[1, 0]))
    cut = GROUP - GROUP // CHUNKS
    most = exchange(lower[:cut])
    rest = exchange(lower[cut:])
    slots[0, 6] = swap(after(slots[0, 4], lower, slots[1, 4]), "img", 2)
    cross(6, slots[1, 2])
    upper = share(by_member(after(raw, slots[0, 6], slots[1, 2]), 0, parts))

    for (j, r), value in list(slots.items()):
        slots[j, r + 1] = swap(value, "img", 1)
    width = -(-side // 16) * 16
    image = jnp.zeros((chans, GROUP * rows + 3, width, depth), activations.dtype)
    for (j, r), value in slots.items():
        owner = rank ^ r
        start = owner * rows + (owner >= GROUP // 2).astype(jnp.int32)
        image = lax.dynamic_update_slice(image, value[None], (mine ^ j, start, 0, 0))

    scalars = jnp.stack([group * GROUP * rows, group]).astype(jnp.int32)
    bias = lax.dynamic_slice_in_dim(channel_bias, rank * split, split)[None]
    own = lambda s: s[1]
    mine_first = [(own, 0, lower, lower.shape, lambda s: (0, 0, 0, 0))]
    every = [
        (lambda s, p=p: p, 0, upper, (GROUP, 3, shard, split), lambda s, p=p: (0, p, 0, 0))
        for p in range(parts)
    ]

    def foreign(array, start):
        block = (None, *array.shape[1:])
        return [
            (
                lambda s, j=j: s[1] ^ j,
                start,
                array,
                block,
                lambda s, j=j: (s[1] ^ j, 0, 0, 0, 0),
            )
            for j in range(1, parts)
        ]

    acc = conv_call((1, 2), mine_first, scalars, image)
    acc = conv_call((0,), every, scalars, image, acc)
    acc = conv_call((1, 2), foreign(most, 0), scalars, image, acc)
    out = conv_call((1, 2), foreign(rest, cut), scalars, image, acc, bias)
    out = share(out).reshape(GROUP, rows, side, split)
    return jnp.moveaxis(out, 0, 2).reshape(rows, side, out_local)


def solution(mesh):
    placed = (P("img", None, "ch"), P(None, None, "img", "ch"), P("ch"))
    return jax.shard_map(
        local, mesh=mesh, in_specs=placed, out_specs=P("img", None, "ch"), check_vma=False
    )
```

```python
import jax
import jax.numpy as jnp
from jax import lax
from jax.experimental import pallas as pl
from jax.experimental.pallas import tpu as pltpu
from jax.sharding import PartitionSpec as P

SIDE = 56
GROUP = 8
TILE = 8
CHUNKS = 4


def swap(array, axis, bit):
    size = lax.axis_size(axis)
    return lax.ppermute(array, axis, [(i, i ^ bit) for i in range(size)])


def after(array, *others):
    return lax.optimization_barrier((array, *others))[0]


def conv_call(taps, pieces, scalars, image, acc=None, bias=None):
    blocks, padded_rows, width, depth = image.shape
    shard, out_width = pieces[0][2].shape[-2:]
    row_count = padded_rows - 3
    offsets = list(dict.fromkeys(piece[0] for piece in pieces))
    per_group = GROUP * shard // depth
    final = bias is not None
    assert row_count % TILE == 0 and SIDE % TILE == 0

    windows = {}
    for offset in offsets:
        ranges = [(start, start + block[-4]) for o, start, _, block, _ in pieces if o == offset]
        low, high = min(a for a, _ in ranges) * shard, max(b for _, b in ranges) * shard
        if low // depth == (high - 1) // depth:
            windows[offset] = (1, low // depth, high - low, low % depth)
        else:
            windows[offset] = (per_group, 0, depth, 0)

    def body(scalars_ref, *refs):
        refs = list(refs)
        images = {}
        for offset in offsets:
            images[offset] = refs.pop(0), *(refs.pop(0) for v in taps if v != 1)
        weights = [refs.pop(0) for _ in pieces]
        acc_ref = refs.pop(0) if acc is not None else None
        bias_ref = refs.pop(0) if final else None
        out = refs.pop(0)

        operands, columns = [], []
        for (offset, start, _, block, _), weight in zip(pieces, weights):
            count, first_block, size, first_lane = windows[offset]
            main, *outer = images[offset]
            at, lanes = 0, block[-4] * shard
            while at < lanes:
                inner, lane = divmod(start * shard + at, depth)
                inner, lane = inner - first_block, lane - first_lane
                length = min(size - lane, lanes - at)
                window = pl.ds(lane, length)
                edges = list(outer)
                for index, vertical in enumerate(taps):
                    rows = main[inner, :, :, window]
                    if vertical == 0:
                        rows = jnp.concatenate(
                            [edges.pop(0)[inner, :, :, window], rows[:-1]], axis=0
                        )
                    if vertical == 2:
                        rows = jnp.concatenate(
                            [rows[1:], edges.pop(0)[inner, :, :, window]], axis=0
                        )
                    operands.append(rows.reshape(TILE * width, length))
                    members = pl.ds(at // shard, length // shard)
                    columns.append(
                        [
                            weight[members, 3 * index + b].reshape(length, out_width)
                            for b in range(3)
                        ]
                    )
                at += length
        operand = jnp.concatenate(operands, axis=1)
        total = None
        for horizontal in range(3):
            value = jnp.dot(
                operand,
                jnp.concatenate([c[horizontal] for c in columns], axis=0),
                preferred_element_type=jnp.float32,
            ).reshape(TILE, width, out_width)
            if horizontal != 1:
                value = pltpu.roll(value, (1 - horizontal) % width, 1)
            total = value if total is None else total + value
        if acc_ref is not None:
            total = total + acc_ref[...]
        if final:
            total = (total + bias_ref[...].reshape(1, 1, -1))[:, : out.shape[1]]
        out[...] = total.astype(out.dtype)

    def image_spec(offset, vertical):
        count, first_block, size, first_lane = windows[offset]
        rows = TILE if vertical == 1 else 1

        def place(t, s):
            row = t * TILE + 1
            if vertical == 0:
                row = jnp.where((s[0] + t * TILE) % SIDE == 0, row_count + 2, row - 1)
            if vertical == 2:
                row = jnp.where((s[0] + (t + 1) * TILE) % SIDE == 0, row_count + 2, row + TILE)
            return (offset(s) * per_group + first_block, row, 0, first_lane)

        return pl.BlockSpec(tuple(pl.Element(n) for n in (count, rows, width, size)), place)

    out_cols = SIDE if final else width
    in_specs, operands = [], []
    for offset in offsets:
        for vertical in [1] + [v for v in taps if v != 1]:
            in_specs.append(image_spec(offset, vertical))
            operands.append(image)
    for _, _, array, block, place in pieces:
        in_specs.append(pl.BlockSpec(block, lambda t, s, place=place: place(s)))
        operands.append(array)
    if acc is not None:
        in_specs.append(pl.BlockSpec((TILE, width, out_width), lambda t, s: (t, 0, 0)))
        operands.append(acc)
    if final:
        in_specs.append(pl.BlockSpec((1, out_width), lambda t, s: (0, 0)))
        operands.append(bias)
    return pl.pallas_call(
        body,
        grid_spec=pltpu.PrefetchScalarGridSpec(
            num_scalar_prefetch=1,
            grid=(row_count // TILE,),
            in_specs=in_specs,
            out_specs=pl.BlockSpec((TILE, out_cols, out_width), lambda t, s: (t, 0, 0)),
        ),
        out_shape=jax.ShapeDtypeStruct(
            (row_count, out_cols, out_width), jnp.bfloat16 if final else jnp.float32
        ),
        compiler_params=pltpu.CompilerParams(vmem_limit_bytes=40 * 1024 * 1024),
        cost_estimate=pl.CostEstimate(flops=1024, bytes_accessed=1024, transcendentals=0),
    )(scalars, *operands)


def by_member(filters, first, count):
    _, across, shard, out_local = filters.shape
    split = out_local // GROUP
    if split % 128:
        taps = filters[first : first + count].reshape(count * across, shard, out_local)
        return jnp.stack([taps[..., r * split : (r + 1) * split] for r in range(GROUP)])

    def body(taps, out):
        for r in range(GROUP):
            out[r, 0] = taps[0, 0, :, r * split : (r + 1) * split]

    return pl.pallas_call(
        body,
        grid=(count, across),
        in_specs=[pl.BlockSpec((1, 1, shard, out_local), lambda v, b: (first + v, b, 0, 0))],
        out_specs=pl.BlockSpec(
            (GROUP, 1, shard, split), lambda v, b: (0, v * across + b, 0, 0)
        ),
        out_shape=jax.ShapeDtypeStruct((GROUP, count * across, shard, split), filters.dtype),
    )(filters)


def local(activations, filters, channel_bias):
    rows, side, depth = activations.shape
    shard, out_local = filters.shape[2:]
    size, chans = lax.axis_size("img"), lax.axis_size("ch")
    me, mine = lax.axis_index("img"), lax.axis_index("ch")
    parts = size // GROUP
    group, rank = me // GROUP, me % GROUP
    members = [[g * GROUP + r for r in range(GROUP)] for g in range(parts)]
    split = out_local // GROUP

    def share(taps):
        return lax.all_to_all(taps, "img", 0, 0, axis_index_groups=members, tiled=True)

    def exchange(array):
        groups = [[g * GROUP + r for g in range(parts)] for r in range(GROUP)]
        return lax.all_gather(array, "img", axis_index_groups=groups)

    first, activations = lax.optimization_barrier((filters[0], activations))
    raw = exchange(first)

    ups = [(i, i + 1) for i in range(size - 1)]
    above = lax.ppermute(activations[-1:], "img", ups)
    below = lax.ppermute(activations[:1], "img", [(j, i) for i, j in ups])
    piece = jnp.where(
        rank >= GROUP // 2,
        jnp.concatenate([activations, below], axis=0),
        jnp.concatenate([above, activations], axis=0),
    )
    slots = {(0, 0): piece}

    def cross(r, *others):
        sent = after(slots[0, r], *others) if others else slots[0, r]
        for j in range(1, chans):
            slots[j, r] = swap(sent, "ch", j)

    cross(0)
    slots[0, 4] = swap(piece, "img", 4)
    slots[0, 2] = swap(piece, "img", 2)

    ready = slots[0, 4], slots[0, 2], slots[1, 0]
    lower = share(after(by_member(filters, 1, 2), *ready))
    cross(4, *ready)
    cross(2, *ready)
    slots[0, 6] = swap(after(slots[0, 4], *ready), "img", 2)
    ready = lower, raw, slots[1, 4], slots[1, 2], slots[0, 6]
    step = GROUP // CHUNKS
    received = []

    def exchange_chunks(chunks, *others):
        for chunk in chunks:
            sent = after(lower[chunk * step : (chunk + 1) * step], *others)
            for j in range(1, parts):
                received.append((j, chunk * step, swap(sent, "img", GROUP * j)))

    exchange_chunks(range(CHUNKS // 2), *ready)
    cross(6, *ready)
    upper = share(by_member(after(raw, *ready), 0, parts))
    for (j, r), value in list(slots.items()):
        slots[j, r + 1] = swap(value, "img", 1)
    ready = [array for _, _, array in received] + list(slots.values())
    exchange_chunks(range(CHUNKS // 2, CHUNKS), *ready)

    width = -(-side // 16) * 16
    image = jnp.zeros((chans, GROUP * rows + 3, width, depth), activations.dtype)
    for (j, r), value in slots.items():
        owner = rank ^ r
        start = owner * rows + (owner >= GROUP // 2).astype(jnp.int32)
        image = lax.dynamic_update_slice(image, value[None], (mine ^ j, start, 0, 0))

    scalars = jnp.stack([group * GROUP * rows, group]).astype(jnp.int32)
    bias = lax.dynamic_slice_in_dim(channel_bias, rank * split, split)[None]
    own = lambda s: s[1]
    half = len(received) // 2
    mine_first = [(own, 0, lower, lower.shape, lambda s: (0, 0, 0, 0))]
    every = [
        (lambda s, p=p: p, 0, upper, (GROUP, 3, shard, split), lambda s, p=p: (0, p, 0, 0))
        for p in range(parts)
    ]

    def foreign(arrays):
        return [
            (lambda s, j=j: s[1] ^ j, start, array, array.shape, lambda s: (0, 0, 0, 0))
            for j, start, array in arrays
        ]

    acc = conv_call((1, 2), mine_first, scalars, image)
    acc = conv_call((0,), every, scalars, image, acc)
    acc = conv_call((1, 2), foreign(received[:half]), scalars, image, acc)
    out = conv_call((1, 2), foreign(received[half:]), scalars, image, acc, bias)
    out = share(out).reshape(GROUP, rows, side, split)
    return jnp.moveaxis(out, 0, 2).reshape(rows, side, out_local)


def solution(mesh):
    placed = (P("img", None, "ch"), P(None, None, "img", "ch"), P("ch"))
    return jax.shard_map(
        local, mesh=mesh, in_specs=placed, out_specs=P("img", None, "ch"), check_vma=False
    )
```

```python
import jax
import jax.numpy as jnp
from jax import lax
from jax.experimental import pallas as pl
from jax.experimental.pallas import tpu as pltpu
from jax.sharding import PartitionSpec as P

SIDE = 56
GROUP = 8
TILE = 8
CHUNKS = 4


def swap(array, axis, bit):
    size = lax.axis_size(axis)
    return lax.ppermute(array, axis, [(i, i ^ bit) for i in range(size)])


def after(array, *others):
    return lax.optimization_barrier((array, *others))[0]


def conv_call(taps, pieces, scalars, image, acc=None, bias=None):
    blocks, padded_rows, width, depth = image.shape
    shard, out_width = pieces[0][2].shape[-2:]
    row_count = padded_rows - 3
    offsets = list(dict.fromkeys(piece[0] for piece in pieces))
    per_group = GROUP * shard // depth
    final = bias is not None
    assert row_count % TILE == 0 and SIDE % TILE == 0

    windows = {}
    for offset in offsets:
        ranges = [(start, start + block[-4]) for o, start, _, block, _ in pieces if o == offset]
        low, high = min(a for a, _ in ranges) * shard, max(b for _, b in ranges) * shard
        if low // depth == (high - 1) // depth:
            windows[offset] = (1, low // depth, high - low, low % depth)
        else:
            windows[offset] = (per_group, 0, depth, 0)

    def body(scalars_ref, *refs):
        refs = list(refs)
        images = {}
        for offset in offsets:
            images[offset] = refs.pop(0), *(refs.pop(0) for v in taps if v != 1)
        weights = [refs.pop(0) for _ in pieces]
        acc_ref = refs.pop(0) if acc is not None else None
        bias_ref = refs.pop(0) if final else None
        out = refs.pop(0)

        operands, columns = [], []
        for (offset, start, _, block, _), weight in zip(pieces, weights):
            count, first_block, size, first_lane = windows[offset]
            main, *outer = images[offset]
            at, lanes = 0, block[-4] * shard
            while at < lanes:
                inner, lane = divmod(start * shard + at, depth)
                inner, lane = inner - first_block, lane - first_lane
                length = min(size - lane, lanes - at)
                window = pl.ds(lane, length)
                edges = list(outer)
                for index, vertical in enumerate(taps):
                    rows = main[inner, :, :, window]
                    if vertical == 0:
                        rows = jnp.concatenate(
                            [edges.pop(0)[inner, :, :, window], rows[:-1]], axis=0
                        )
                    if vertical == 2:
                        rows = jnp.concatenate(
                            [rows[1:], edges.pop(0)[inner, :, :, window]], axis=0
                        )
                    operands.append(rows.reshape(TILE * width, length))
                    members = pl.ds(at // shard, length // shard)
                    columns.append(
                        [
                            weight[members, 3 * index + b].reshape(length, out_width)
                            for b in range(3)
                        ]
                    )
                at += length
        operand = jnp.concatenate(operands, axis=1)
        total = None
        for horizontal in range(3):
            value = jnp.dot(
                operand,
                jnp.concatenate([c[horizontal] for c in columns], axis=0),
                preferred_element_type=jnp.float32,
            ).reshape(TILE, width, out_width)
            if horizontal != 1:
                value = pltpu.roll(value, (1 - horizontal) % width, 1)
            total = value if total is None else total + value
        if acc_ref is not None:
            total = total + acc_ref[...]
        if final:
            total = (total + bias_ref[...].reshape(1, 1, -1))[:, : out.shape[1]]
        out[...] = total.astype(out.dtype)

    def image_spec(offset, vertical):
        count, first_block, size, first_lane = windows[offset]
        rows = TILE if vertical == 1 else 1

        def place(t, s):
            row = t * TILE + 1
            if vertical == 0:
                row = jnp.where((s[0] + t * TILE) % SIDE == 0, row_count + 2, row - 1)
            if vertical == 2:
                row = jnp.where((s[0] + (t + 1) * TILE) % SIDE == 0, row_count + 2, row + TILE)
            return (offset(s) * per_group + first_block, row, 0, first_lane)

        return pl.BlockSpec(tuple(pl.Element(n) for n in (count, rows, width, size)), place)

    out_cols = SIDE if final else width
    in_specs, operands = [], []
    for offset in offsets:
        for vertical in [1] + [v for v in taps if v != 1]:
            in_specs.append(image_spec(offset, vertical))
            operands.append(image)
    for _, _, array, block, place in pieces:
        in_specs.append(pl.BlockSpec(block, lambda t, s, place=place: place(s)))
        operands.append(array)
    if acc is not None:
        in_specs.append(pl.BlockSpec((TILE, width, out_width), lambda t, s: (t, 0, 0)))
        operands.append(acc)
    if final:
        in_specs.append(pl.BlockSpec((1, out_width), lambda t, s: (0, 0)))
        operands.append(bias)
    return pl.pallas_call(
        body,
        grid_spec=pltpu.PrefetchScalarGridSpec(
            num_scalar_prefetch=1,
            grid=(row_count // TILE,),
            in_specs=in_specs,
            out_specs=pl.BlockSpec((TILE, out_cols, out_width), lambda t, s: (t, 0, 0)),
        ),
        out_shape=jax.ShapeDtypeStruct(
            (row_count, out_cols, out_width), jnp.bfloat16 if final else jnp.float32
        ),
        compiler_params=pltpu.CompilerParams(vmem_limit_bytes=40 * 1024 * 1024),
        cost_estimate=pl.CostEstimate(flops=1024, bytes_accessed=1024, transcendentals=0),
    )(scalars, *operands)


def by_member(filters, first, count):
    _, across, shard, out_local = filters.shape
    split = out_local // GROUP
    if split % 128:
        taps = filters[first : first + count].reshape(count * across, shard, out_local)
        return jnp.stack([taps[..., r * split : (r + 1) * split] for r in range(GROUP)])

    def body(taps, out):
        for r in range(GROUP):
            out[r, 0] = taps[0, 0, :, r * split : (r + 1) * split]

    return pl.pallas_call(
        body,
        grid=(count, across),
        in_specs=[pl.BlockSpec((1, 1, shard, out_local), lambda v, b: (first + v, b, 0, 0))],
        out_specs=pl.BlockSpec(
            (GROUP, 1, shard, split), lambda v, b: (0, v * across + b, 0, 0)
        ),
        out_shape=jax.ShapeDtypeStruct((GROUP, count * across, shard, split), filters.dtype),
    )(filters)


def local(activations, filters, channel_bias):
    rows, side, depth = activations.shape
    shard, out_local = filters.shape[2:]
    size, chans = lax.axis_size("img"), lax.axis_size("ch")
    me, mine = lax.axis_index("img"), lax.axis_index("ch")
    parts = size // GROUP
    group, rank = me // GROUP, me % GROUP
    members = [[g * GROUP + r for r in range(GROUP)] for g in range(parts)]
    split = out_local // GROUP

    def share(taps):
        return lax.all_to_all(taps, "img", 0, 0, axis_index_groups=members, tiled=True)

    def exchange(array):
        return [swap(array, "img", GROUP * j) for j in range(1, parts)]

    ready = []

    def step(array):
        return after(array, *ready) if ready else array

    first, second = filters[0, :2], filters[0, 2:]
    ups = [(i, i + 1) for i in range(size - 1)]
    above = lax.ppermute(activations[-1:], "img", ups)
    below = lax.ppermute(activations[:1], "img", [(j, i) for i, j in ups])
    piece = jnp.where(
        rank >= GROUP // 2,
        jnp.concatenate([activations, below], axis=0),
        jnp.concatenate([above, activations], axis=0),
    )
    slots = {(0, 0): piece}
    width = -(-side // 16) * 16
    image = jnp.zeros((chans, GROUP * rows + 3, width, depth), activations.dtype)

    def over_ch(r):
        sent = step(slots[0, r])
        for j in range(1, chans):
            slots[j, r] = swap(sent, "ch", j)

    def over_core(keys):
        for j, r in keys:
            slots[j, r + 1] = swap(step(slots[j, r]), "img", 1)

    def place(image, keys):
        for j, r in keys:
            owner = rank ^ r
            start = owner * rows + (owner >= GROUP // 2).astype(jnp.int32)
            image = lax.dynamic_update_slice(image, slots[j, r][None], (mine ^ j, start, 0, 0))
        return image

    others = range(1, chans)

    taken = exchange(first)
    by_rank = by_member(filters, 1, 2)
    over_ch(0)
    slots[0, 4] = swap(piece, "img", 4)
    slots[0, 2] = swap(piece, "img", 2)
    ready = [*taken, slots[0, 4], slots[0, 2], *(slots[j, 0] for j in others), by_rank]

    lower = share(step(by_rank))
    over_ch(4)
    taken_last = exchange(step(second))
    keys = [(0, 0), (0, 4), (0, 2)] + [(j, 0) for j in others]
    over_core(keys)
    image = place(image, keys)
    ready = [lower, *(slots[j, 4] for j in others), *taken_last, image]
    ready += [slots[j, r + 1] for j, r in keys]

    span = GROUP // CHUNKS
    chunks = [lower[c * span : (c + 1) * span] for c in range(CHUNKS)]
    received = [exchange(step(chunks[0]))]
    over_ch(2)
    slots[0, 6] = swap(step(slots[0, 4]), "img", 2)
    image = place(image, [(j, r + 1) for j, r in keys])
    keys = [(j, 4) for j in others]
    over_core(keys)
    image = place(image, keys)
    raw = [filters[0]] + [jnp.concatenate(pair) for pair in zip(taken, taken_last)]
    by_rank = by_member(step(jnp.stack(raw)), 0, parts)
    ready = [*received[0], slots[0, 6], *(slots[j, 2] for j in others), image, by_rank]
    ready += [slots[j, r + 1] for j, r in keys]

    received.append(exchange(step(chunks[1])))
    over_ch(6)
    upper = share(step(by_rank))
    image = place(image, [(j, r + 1) for j, r in keys])
    keys = [(0, 6)] + [(j, 2) for j in others]
    over_core(keys)
    image = place(image, keys)
    image = place(image, [(j, r + 1) for j, r in keys])
    ready = [*received[1], upper, *(slots[j, 6] for j in others), image]

    received.append(exchange(step(chunks[2])))
    keys = [(j, 6) for j in others]
    over_core(keys)
    image = place(image, keys)
    image = place(image, [(j, r + 1) for j, r in keys])

    scalars = jnp.stack([group * GROUP * rows, group]).astype(jnp.int32)
    bias = lax.dynamic_slice_in_dim(channel_bias, rank * split, split)[None]
    own = lambda s: s[1]
    at_start = lambda s: (0, 0, 0, 0)
    every = [
        (lambda s, j=j: s[1] ^ j, 0, upper, (GROUP, 3, shard, split), lambda s, j=j: (0, j, 0, 0))
        for j in range(parts)
    ]
    foreign = [lambda s, j=j: s[1] ^ j for j in range(1, parts)]

    def pieces(chosen):
        return [
            (foreign[j], c * span, array, array.shape, at_start)
            for c in chosen
            for j, array in enumerate(received[c])
        ]

    acc = conv_call((1, 2), [(own, 0, lower, lower.shape, at_start)], scalars, image)

    received.append(exchange(after(chunks[3], acc, *received[2])))
    acc = conv_call((0,), every, scalars, image, acc)
    acc = conv_call((1, 2), pieces((0, 1, 2)), scalars, image, acc)
    out = conv_call((1, 2), pieces((3,)), scalars, image, acc, bias)
    out = share(out).reshape(GROUP, rows, side, split)
    return jnp.moveaxis(out, 0, 2).reshape(rows, side, out_local)


def solution(mesh):
    placed = (P("img", None, "ch"), P(None, None, "img", "ch"), P("ch"))
    return jax.shard_map(
        local, mesh=mesh, in_specs=placed, out_specs=P("img", None, "ch"), check_vma=False
    )
```

```python
import jax
import jax.numpy as jnp
from jax import lax
from jax.experimental import pallas as pl
from jax.experimental.pallas import tpu as pltpu
from jax.sharding import PartitionSpec as P

SIDE = 56
GROUP = 8
TILE = 8


def swap(array, axis, bit):
    size = lax.axis_size(axis)
    return lax.ppermute(array, axis, [(i, i ^ bit) for i in range(size)])


def after(array, *others):
    return lax.optimization_barrier((array, *others))[0]


def conv_call(pieces, scalars, image, acc=None, bias=None):
    blocks, padded_rows, width, depth = image.shape
    shard, out_width = pieces[0][3][-2:]
    row_count = padded_rows - 3
    offsets = list(dict.fromkeys(piece[0] for piece in pieces))
    per_group = GROUP * shard // depth
    final = bias is not None
    assert row_count % TILE == 0 and SIDE % TILE == 0

    edges_of = {
        offset: sorted({v for o, *_, taps in pieces if o == offset for v in taps if v != 1})
        for offset in offsets
    }
    windows = {}
    for offset in offsets:
        ranges = [(start, start + block[-4]) for o, start, _, block, *_ in pieces if o == offset]
        low, high = min(a for a, _ in ranges) * shard, max(b for _, b in ranges) * shard
        if low // depth == (high - 1) // depth:
            windows[offset] = (1, low // depth, high - low, low % depth)
        else:
            windows[offset] = (per_group, 0, depth, 0)

    def body(scalars_ref, *refs):
        refs = list(refs)
        images = {}
        for offset in offsets:
            images[offset] = refs.pop(0), {v: refs.pop(0) for v in edges_of[offset]}
        weights = [refs.pop(0) for _ in pieces]
        acc_ref = refs.pop(0) if acc is not None else None
        bias_ref = refs.pop(0) if final else None
        out = refs.pop(0)

        operands, columns = [], []
        for (offset, start, _, block, _, taps), weight in zip(pieces, weights):
            count, first_block, size, first_lane = windows[offset]
            main, edges = images[offset]
            at, lanes = 0, block[-4] * shard
            while at < lanes:
                inner, lane = divmod(start * shard + at, depth)
                inner, lane = inner - first_block, lane - first_lane
                length = min(size - lane, lanes - at)
                window = pl.ds(lane, length)
                for index, vertical in enumerate(taps):
                    rows = main[inner, :, :, window]
                    if vertical == 0:
                        rows = jnp.concatenate(
                            [edges[0][inner, :, :, window], rows[:-1]], axis=0
                        )
                    if vertical == 2:
                        rows = jnp.concatenate(
                            [rows[1:], edges[2][inner, :, :, window]], axis=0
                        )
                    operands.append(rows.reshape(TILE * width, length))
                    members = pl.ds(at // shard, length // shard)
                    columns.append(
                        [
                            weight[members, 3 * index + b].reshape(length, out_width)
                            for b in range(3)
                        ]
                    )
                at += length
        operand = jnp.concatenate(operands, axis=1)
        total = None
        for horizontal in range(3):
            value = jnp.dot(
                operand,
                jnp.concatenate([c[horizontal] for c in columns], axis=0),
                preferred_element_type=jnp.float32,
            ).reshape(TILE, width, out_width)
            if horizontal != 1:
                value = pltpu.roll(value, (1 - horizontal) % width, 1)
            total = value if total is None else total + value
        if acc_ref is not None:
            total = total + acc_ref[...]
        if final:
            total = (total + bias_ref[...].reshape(1, 1, -1))[:, : out.shape[1]]
        out[...] = total.astype(out.dtype)

    def image_spec(offset, vertical):
        count, first_block, size, first_lane = windows[offset]
        rows = TILE if vertical == 1 else 1

        def place(t, s):
            row = t * TILE + 1
            if vertical == 0:
                row = jnp.where((s[0] + t * TILE) % SIDE == 0, row_count + 2, row - 1)
            if vertical == 2:
                row = jnp.where((s[0] + (t + 1) * TILE) % SIDE == 0, row_count + 2, row + TILE)
            return (offset(s) * per_group + first_block, row, 0, first_lane)

        return pl.BlockSpec(tuple(pl.Element(n) for n in (count, rows, width, size)), place)

    out_cols = SIDE if final else width
    in_specs, operands = [], []
    for offset in offsets:
        for vertical in [1] + edges_of[offset]:
            in_specs.append(image_spec(offset, vertical))
            operands.append(image)
    for _, _, array, block, place, _ in pieces:
        in_specs.append(pl.BlockSpec(block, lambda t, s, place=place: place(s)))
        operands.append(array)
    if acc is not None:
        in_specs.append(pl.BlockSpec((TILE, width, out_width), lambda t, s: (t, 0, 0)))
        operands.append(acc)
    if final:
        in_specs.append(pl.BlockSpec((1, out_width), lambda t, s: (0, 0)))
        operands.append(bias)
    return pl.pallas_call(
        body,
        grid_spec=pltpu.PrefetchScalarGridSpec(
            num_scalar_prefetch=1,
            grid=(row_count // TILE,),
            in_specs=in_specs,
            out_specs=pl.BlockSpec((TILE, out_cols, out_width), lambda t, s: (t, 0, 0)),
        ),
        out_shape=jax.ShapeDtypeStruct(
            (row_count, out_cols, out_width), jnp.bfloat16 if final else jnp.float32
        ),
        compiler_params=pltpu.CompilerParams(vmem_limit_bytes=40 * 1024 * 1024),
        cost_estimate=pl.CostEstimate(flops=1024, bytes_accessed=1024, transcendentals=0),
    )(scalars, *operands)


def by_member(filters, first, count):
    _, across, shard, out_local = filters.shape
    split = out_local // GROUP
    if split % 128:
        taps = filters[first : first + count].reshape(count * across, shard, out_local)
        return jnp.stack([taps[..., r * split : (r + 1) * split] for r in range(GROUP)])

    def body(taps, out):
        for r in range(GROUP):
            out[r, 0] = taps[0, 0, :, r * split : (r + 1) * split]

    return pl.pallas_call(
        body,
        grid=(count, across),
        in_specs=[pl.BlockSpec((1, 1, shard, out_local), lambda v, b: (first + v, b, 0, 0))],
        out_specs=pl.BlockSpec(
            (GROUP, 1, shard, split), lambda v, b: (0, v * across + b, 0, 0)
        ),
        out_shape=jax.ShapeDtypeStruct((GROUP, count * across, shard, split), filters.dtype),
    )(filters)


def local(activations, filters, channel_bias):
    rows, side, depth = activations.shape
    shard, out_local = filters.shape[2:]
    size, chans = lax.axis_size("img"), lax.axis_size("ch")
    me, mine = lax.axis_index("img"), lax.axis_index("ch")
    parts = size // GROUP
    group, rank = me // GROUP, me % GROUP
    members = [[g * GROUP + r for r in range(GROUP)] for g in range(parts)]
    split = out_local // GROUP

    def share(taps):
        return lax.all_to_all(taps, "img", 0, 0, axis_index_groups=members, tiled=True)

    def exchange(array):
        return [swap(array, "img", GROUP * j) for j in range(1, parts)]

    ready = []

    def step(array):
        return after(array, *ready) if ready else array

    first, activations = lax.optimization_barrier((filters[0, :2], activations))
    second = filters[0, 2:]
    ups = [(i, i + 1) for i in range(size - 1)]
    above = lax.ppermute(activations[-1:], "img", ups)
    below = lax.ppermute(activations[:1], "img", [(j, i) for i, j in ups])
    piece = jnp.where(
        rank >= GROUP // 2,
        jnp.concatenate([activations, below], axis=0),
        jnp.concatenate([above, activations], axis=0),
    )
    slots = {(0, 0): piece}
    width = -(-side // 16) * 16
    image = jnp.zeros((chans, GROUP * rows + 3, width, depth), activations.dtype)

    def over_ch(r):
        sent = step(slots[0, r])
        for j in range(1, chans):
            slots[j, r] = swap(sent, "ch", j)

    def over_core(keys):
        for j, r in keys:
            slots[j, r + 1] = swap(step(slots[j, r]), "img", 1)

    def place(image, keys):
        for j, r in keys:
            owner = rank ^ r
            start = owner * rows + (owner >= GROUP // 2).astype(jnp.int32)
            image = lax.dynamic_update_slice(image, slots[j, r][None], (mine ^ j, start, 0, 0))
        return image

    others = range(1, chans)

    taken = exchange(first)
    by_rank = by_member(filters, 1, 2)
    over_ch(0)
    slots[0, 4] = swap(piece, "img", 4)
    slots[0, 2] = swap(piece, "img", 2)
    ready = [*taken, slots[0, 4], slots[0, 2], *(slots[j, 0] for j in others), by_rank]

    lower = share(step(by_rank))
    over_ch(4)
    taken_last = exchange(step(second))
    keys = [(0, 0), (0, 4), (0, 2)] + [(j, 0) for j in others]
    over_core(keys)
    image = place(image, keys)
    ready = [lower, *(slots[j, 4] for j in others), *taken_last]
    ready += [slots[j, r + 1] for j, r in keys]

    cuts = (0, GROUP // 4, GROUP // 2, GROUP)
    chunks = [lower[a:b] for a, b in zip(cuts, cuts[1:])]
    received = [exchange(step(chunks[0]))]
    over_ch(2)
    slots[0, 6] = swap(step(slots[0, 4]), "img", 2)
    image = place(image, [(j, r + 1) for j, r in keys])
    keys = [(j, 4) for j in others]
    over_core(keys)
    image = place(image, keys)
    raw = [filters[0]] + [
        jnp.concatenate([step(a), step(b)]) for a, b in zip(taken, taken_last)
    ]
    by_rank = by_member(jnp.stack(raw), 0, parts)
    ready = [*received[0], slots[0, 6], *(slots[j, 2] for j in others), image, by_rank]
    ready += [slots[j, r + 1] for j, r in keys]

    received.append(exchange(step(chunks[1])))
    over_ch(6)
    upper = share(step(by_rank))
    image = place(image, [(j, r + 1) for j, r in keys])
    keys = [(0, 6)] + [(j, 2) for j in others]
    over_core(keys)
    image = place(image, keys)
    image = place(image, [(j, r + 1) for j, r in keys])
    ready = [*received[1], *(slots[j, 6] for j in others), image]

    received.append(exchange(step(chunks[2])))
    keys = [(j, 6) for j in others]
    over_core(keys)
    image = place(image, keys)
    image = place(image, [(j, r + 1) for j, r in keys])

    scalars = jnp.stack([group * GROUP * rows, group]).astype(jnp.int32)
    bias = lax.dynamic_slice_in_dim(channel_bias, rank * split, split)[None]
    which = [lambda s, j=j: s[1] ^ j for j in range(parts)]
    at_start = lambda s: (0, 0, 0, 0)
    every = [
        (which[j], 0, upper, (GROUP, 3, shard, split), lambda s, j=j: (0, j, 0, 0), (0,))
        for j in range(parts)
    ]

    def pieces(chosen):
        return [
            (which[j], cuts[c], array, array.shape, at_start, (1, 2))
            for c in chosen
            for j, array in enumerate(received[c], 1)
        ]

    acc = conv_call([(which[0], 0, lower, lower.shape, at_start, (1, 2))], scalars, image)
    acc = conv_call(every + pieces((0, 1)), scalars, image, acc)
    out = conv_call(pieces((2,)), scalars, image, acc, bias)
    out = share(out).reshape(GROUP, rows, side, split)
    return jnp.moveaxis(out, 0, 2).reshape(rows, side, out_local)


def solution(mesh):
    placed = (P("img", None, "ch"), P(None, None, "img", "ch"), P("ch"))
    return jax.shard_map(
        local, mesh=mesh, in_specs=placed, out_specs=P("img", None, "ch"), check_vma=False
    )
```

```python
import jax
import jax.numpy as jnp
from jax import lax
from jax.experimental import pallas as pl
from jax.experimental.pallas import tpu as pltpu
from jax.sharding import PartitionSpec as P

SIDE = 56
GROUP = 8
TILE = 8


def swap(array, axis, bit):
    size = lax.axis_size(axis)
    return lax.ppermute(array, axis, [(i, i ^ bit) for i in range(size)])


def after(array, *others):
    return lax.optimization_barrier((array, *others))[0]


def conv_call(pieces, scalars, image, acc=None, bias=None):
    blocks, padded_rows, width, depth = image.shape
    shard, out_width = pieces[0][3][-2:]
    row_count = padded_rows - 3
    offsets = list(dict.fromkeys(piece[0] for piece in pieces))
    per_group = GROUP * shard // depth
    final = bias is not None
    assert row_count % TILE == 0 and SIDE % TILE == 0

    edges_of = {
        offset: sorted({v for o, *_, taps in pieces if o == offset for v in taps if v != 1})
        for offset in offsets
    }
    windows = {}
    for offset in offsets:
        ranges = [(start, start + block[-4]) for o, start, _, block, *_ in pieces if o == offset]
        low, high = min(a for a, _ in ranges) * shard, max(b for _, b in ranges) * shard
        if low // depth == (high - 1) // depth:
            windows[offset] = (1, low // depth, high - low, low % depth)
        else:
            windows[offset] = (per_group, 0, depth, 0)

    def body(scalars_ref, *refs):
        refs = list(refs)
        images = {}
        for offset in offsets:
            images[offset] = refs.pop(0), {v: refs.pop(0) for v in edges_of[offset]}
        weights = [refs.pop(0) for _ in pieces]
        acc_ref = refs.pop(0) if acc is not None else None
        bias_ref = refs.pop(0) if final else None
        out = refs.pop(0)

        operands, columns = [], []
        for (offset, start, _, block, _, taps), weight in zip(pieces, weights):
            count, first_block, size, first_lane = windows[offset]
            main, edges = images[offset]
            at, lanes = 0, block[-4] * shard
            while at < lanes:
                inner, lane = divmod(start * shard + at, depth)
                inner, lane = inner - first_block, lane - first_lane
                length = min(size - lane, lanes - at)
                window = pl.ds(lane, length)
                for index, vertical in enumerate(taps):
                    rows = main[inner, :, :, window]
                    if vertical == 0:
                        rows = jnp.concatenate(
                            [edges[0][inner, :, :, window], rows[:-1]], axis=0
                        )
                    if vertical == 2:
                        rows = jnp.concatenate(
                            [rows[1:], edges[2][inner, :, :, window]], axis=0
                        )
                    operands.append(rows.reshape(TILE * width, length))
                    members = pl.ds(at // shard, length // shard)
                    columns.append(
                        [
                            weight[members, 3 * index + b].reshape(length, out_width)
                            for b in range(3)
                        ]
                    )
                at += length
        operand = jnp.concatenate(operands, axis=1)
        total = None
        for horizontal in range(3):
            value = jnp.dot(
                operand,
                jnp.concatenate([c[horizontal] for c in columns], axis=0),
                preferred_element_type=jnp.float32,
            ).reshape(TILE, width, out_width)
            if horizontal != 1:
                value = pltpu.roll(value, (1 - horizontal) % width, 1)
            total = value if total is None else total + value
        if acc_ref is not None:
            total = total + acc_ref[...]
        if final:
            total = (total + bias_ref[...].reshape(1, 1, -1))[:, : out.shape[1]]
        out[...] = total.astype(out.dtype)

    def image_spec(offset, vertical):
        count, first_block, size, first_lane = windows[offset]
        rows = TILE if vertical == 1 else 1

        def place(t, s):
            row = t * TILE + 1
            if vertical == 0:
                row = jnp.where((s[0] + t * TILE) % SIDE == 0, row_count + 2, row - 1)
            if vertical == 2:
                row = jnp.where((s[0] + (t + 1) * TILE) % SIDE == 0, row_count + 2, row + TILE)
            return (offset(s) * per_group + first_block, row, 0, first_lane)

        return pl.BlockSpec(tuple(pl.Element(n) for n in (count, rows, width, size)), place)

    out_cols = SIDE if final else width
    in_specs, operands = [], []
    for offset in offsets:
        for vertical in [1] + edges_of[offset]:
            in_specs.append(image_spec(offset, vertical))
            operands.append(image)
    for _, _, array, block, place, _ in pieces:
        in_specs.append(pl.BlockSpec(block, lambda t, s, place=place: place(s)))
        operands.append(array)
    if acc is not None:
        in_specs.append(pl.BlockSpec((TILE, width, out_width), lambda t, s: (t, 0, 0)))
        operands.append(acc)
    if final:
        in_specs.append(pl.BlockSpec((1, out_width), lambda t, s: (0, 0)))
        operands.append(bias)
    return pl.pallas_call(
        body,
        grid_spec=pltpu.PrefetchScalarGridSpec(
            num_scalar_prefetch=1,
            grid=(row_count // TILE,),
            in_specs=in_specs,
            out_specs=pl.BlockSpec((TILE, out_cols, out_width), lambda t, s: (t, 0, 0)),
        ),
        out_shape=jax.ShapeDtypeStruct(
            (row_count, out_cols, out_width), jnp.bfloat16 if final else jnp.float32
        ),
        compiler_params=pltpu.CompilerParams(vmem_limit_bytes=40 * 1024 * 1024),
        cost_estimate=pl.CostEstimate(flops=1024, bytes_accessed=1024, transcendentals=0),
    )(scalars, *operands)


def by_member(filters, first, count):
    _, across, shard, out_local = filters.shape
    split = out_local // GROUP
    if split % 128:
        taps = filters[first : first + count].reshape(count * across, shard, out_local)
        return jnp.stack([taps[..., r * split : (r + 1) * split] for r in range(GROUP)])

    def body(taps, out):
        for r in range(GROUP):
            out[r, 0] = taps[0, 0, :, r * split : (r + 1) * split]

    return pl.pallas_call(
        body,
        grid=(count, across),
        in_specs=[pl.BlockSpec((1, 1, shard, out_local), lambda v, b: (first + v, b, 0, 0))],
        out_specs=pl.BlockSpec(
            (GROUP, 1, shard, split), lambda v, b: (0, v * across + b, 0, 0)
        ),
        out_shape=jax.ShapeDtypeStruct((GROUP, count * across, shard, split), filters.dtype),
    )(filters)


def local(activations, filters, channel_bias):
    rows, side, depth = activations.shape
    shard, out_local = filters.shape[2:]
    size, chans = lax.axis_size("img"), lax.axis_size("ch")
    me, mine = lax.axis_index("img"), lax.axis_index("ch")
    parts = size // GROUP
    group, rank = me // GROUP, me % GROUP
    members = [[g * GROUP + r for r in range(GROUP)] for g in range(parts)]
    split = out_local // GROUP

    def share(taps):
        return lax.all_to_all(taps, "img", 0, 0, axis_index_groups=members, tiled=True)

    def exchange(array):
        return [swap(array, "img", GROUP * j) for j in range(1, parts)]

    ready = []

    def step(array):
        return after(array, *ready) if ready else array

    first, activations = lax.optimization_barrier((filters[0, :1], activations))
    taken_first = exchange(first)
    taken = exchange(after(filters[0, 1:], *taken_first))

    ups = [(i, i + 1) for i in range(size - 1)]
    above = lax.ppermute(activations[-1:], "img", ups)
    below = lax.ppermute(activations[:1], "img", [(j, i) for i, j in ups])
    piece = jnp.where(
        rank >= GROUP // 2,
        jnp.concatenate([activations, below], axis=0),
        jnp.concatenate([above, activations], axis=0),
    )
    slots = {(0, 0): piece}
    width = -(-side // 16) * 16
    image = jnp.zeros((chans, GROUP * rows + 3, width, depth), activations.dtype)

    def over_ch(r):
        sent = step(slots[0, r])
        for j in range(1, chans):
            slots[j, r] = swap(sent, "ch", j)

    def over_core(keys):
        for j, r in keys:
            slots[j, r + 1] = swap(step(slots[j, r]), "img", 1)

    def place(image, keys):
        for j, r in keys:
            owner = rank ^ r
            start = owner * rows + (owner >= GROUP // 2).astype(jnp.int32)
            image = lax.dynamic_update_slice(image, slots[j, r][None], (mine ^ j, start, 0, 0))
        return image

    others = range(1, chans)

    by_rank = by_member(filters, 2, 1)
    own_mid = share(by_member(filters, 1, 1))
    over_ch(0)
    slots[0, 4] = swap(piece, "img", 4)
    slots[0, 2] = swap(piece, "img", 2)
    ready = [*taken, own_mid, slots[0, 4], slots[0, 2], *(slots[j, 0] for j in others), by_rank]

    taken_mid = exchange(step(own_mid))
    own_low = share(step(by_rank))
    over_ch(4)
    over_ch(2)
    slots[0, 6] = swap(step(slots[0, 4]), "img", 2)
    keys = [(0, 0), (0, 4), (0, 2)] + [(j, 0) for j in others]
    over_core(keys)
    image = place(image, keys)
    raw = [filters[0]] + [
        jnp.concatenate([step(a), step(b)]) for a, b in zip(taken_first, taken)
    ]
    by_rank = by_member(jnp.stack(raw), 0, parts)
    ready = [*taken_mid, own_low, slots[0, 6], by_rank, image]
    ready += [slots[j, r] for j in others for r in (4, 2)]
    ready += [slots[j, r + 1] for j, r in keys]

    taken_low = exchange(step(own_low))
    over_ch(6)
    upper = share(step(by_rank))
    image = place(image, [(j, r + 1) for j, r in keys])
    keys = [(0, 6)] + [(j, r) for j in others for r in (4, 2)]
    over_core(keys)
    image = place(image, keys + [(j, r + 1) for j, r in keys])
    keys = [(j, 6) for j in others]
    ready = []
    over_core(keys)
    image = place(image, keys + [(j, r + 1) for j, r in keys])

    scalars = jnp.stack([group * GROUP * rows, group]).astype(jnp.int32)
    bias = lax.dynamic_slice_in_dim(channel_bias, rank * split, split)[None]
    which = [lambda s, j=j: s[1] ^ j for j in range(parts)]

    def pieces(arrays, vertical):
        return [
            (which[j], 0, array, array.shape, lambda s: (0, 0, 0, 0), (vertical,))
            for j, array in arrays
        ]

    every = [
        (which[j], 0, upper, (GROUP, 3, shard, split), lambda s, j=j: (0, j, 0, 0), (0,))
        for j in range(parts)
    ]
    early = pieces([(0, own_mid), *enumerate(taken_mid, 1)], 1) + pieces([(0, own_low)], 2)
    acc = conv_call(early, scalars, image)
    out = conv_call(every + pieces(enumerate(taken_low, 1), 2), scalars, image, acc, bias)
    out = share(out).reshape(GROUP, rows, side, split)
    return jnp.moveaxis(out, 0, 2).reshape(rows, side, out_local)


def solution(mesh):
    placed = (P("img", None, "ch"), P(None, None, "img", "ch"), P("ch"))
    return jax.shard_map(
        local, mesh=mesh, in_specs=placed, out_specs=P("img", None, "ch"), check_vma=False
    )
```

```python
import jax
import jax.numpy as jnp
from jax import lax
from jax.experimental import pallas as pl
from jax.experimental.pallas import tpu as pltpu
from jax.sharding import PartitionSpec as P

SIDE = 56
GROUP = 8
TILE = 8


def swap(array, axis, bit):
    size = lax.axis_size(axis)
    return lax.ppermute(array, axis, [(i, i ^ bit) for i in range(size)])


def after(array, *others):
    return lax.optimization_barrier((array, *others))[0]


def conv_call(pieces, scalars, image, acc=None, bias=None):
    blocks, padded_rows, width, depth = image.shape
    shard, out_width = pieces[0][3][-2:]
    row_count = padded_rows - 3
    offsets = list(dict.fromkeys(piece[0] for piece in pieces))
    per_group = GROUP * shard // depth
    final = bias is not None
    assert row_count % TILE == 0 and SIDE % TILE == 0

    edges_of = {
        offset: sorted({v for o, *_, taps in pieces if o == offset for v in taps if v != 1})
        for offset in offsets
    }
    windows = {}
    for offset in offsets:
        ranges = [(start, start + block[-4]) for o, start, _, block, *_ in pieces if o == offset]
        low, high = min(a for a, _ in ranges) * shard, max(b for _, b in ranges) * shard
        if low // depth == (high - 1) // depth:
            windows[offset] = (1, low // depth, high - low, low % depth)
        else:
            windows[offset] = (per_group, 0, depth, 0)

    def body(scalars_ref, *refs):
        refs = list(refs)
        images = {}
        for offset in offsets:
            images[offset] = refs.pop(0), {v: refs.pop(0) for v in edges_of[offset]}
        weights = [refs.pop(0) for _ in pieces]
        acc_ref = refs.pop(0) if acc is not None else None
        bias_ref = refs.pop(0) if final else None
        out = refs.pop(0)

        operands, columns = [], []
        for (offset, start, _, block, _, taps), weight in zip(pieces, weights):
            count, first_block, size, first_lane = windows[offset]
            main, edges = images[offset]
            at, lanes = 0, block[-4] * shard
            while at < lanes:
                inner, lane = divmod(start * shard + at, depth)
                inner, lane = inner - first_block, lane - first_lane
                length = min(size - lane, lanes - at)
                window = pl.ds(lane, length)
                for index, vertical in enumerate(taps):
                    rows = main[inner, :, :, window]
                    if vertical == 0:
                        rows = jnp.concatenate(
                            [edges[0][inner, :, :, window], rows[:-1]], axis=0
                        )
                    if vertical == 2:
                        rows = jnp.concatenate(
                            [rows[1:], edges[2][inner, :, :, window]], axis=0
                        )
                    operands.append(rows.reshape(TILE * width, length))
                    members = pl.ds(at // shard, length // shard)
                    columns.append(
                        [
                            weight[members, 3 * index + b].reshape(length, out_width)
                            for b in range(3)
                        ]
                    )
                at += length
        operand = jnp.concatenate(operands, axis=1)
        total = None
        for horizontal in range(3):
            value = jnp.dot(
                operand,
                jnp.concatenate([c[horizontal] for c in columns], axis=0),
                preferred_element_type=jnp.float32,
            ).reshape(TILE, width, out_width)
            if horizontal != 1:
                value = pltpu.roll(value, (1 - horizontal) % width, 1)
            total = value if total is None else total + value
        if acc_ref is not None:
            total = total + acc_ref[...]
        if final:
            total = (total + bias_ref[...].reshape(1, 1, -1))[:, : out.shape[1]]
        out[...] = total.astype(out.dtype)

    def image_spec(offset, vertical):
        count, first_block, size, first_lane = windows[offset]
        rows = TILE if vertical == 1 else 1

        def place(t, s):
            row = t * TILE + 1
            if vertical == 0:
                row = jnp.where((s[0] + t * TILE) % SIDE == 0, row_count + 2, row - 1)
            if vertical == 2:
                row = jnp.where((s[0] + (t + 1) * TILE) % SIDE == 0, row_count + 2, row + TILE)
            return (offset(s) * per_group + first_block, row, 0, first_lane)

        return pl.BlockSpec(tuple(pl.Element(n) for n in (count, rows, width, size)), place)

    out_cols = SIDE if final else width
    in_specs, operands = [], []
    for offset in offsets:
        for vertical in [1] + edges_of[offset]:
            in_specs.append(image_spec(offset, vertical))
            operands.append(image)
    for _, _, array, block, place, _ in pieces:
        in_specs.append(pl.BlockSpec(block, lambda t, s, place=place: place(s)))
        operands.append(array)
    if acc is not None:
        in_specs.append(pl.BlockSpec((TILE, width, out_width), lambda t, s: (t, 0, 0)))
        operands.append(acc)
    if final:
        in_specs.append(pl.BlockSpec((1, out_width), lambda t, s: (0, 0)))
        operands.append(bias)
    return pl.pallas_call(
        body,
        grid_spec=pltpu.PrefetchScalarGridSpec(
            num_scalar_prefetch=1,
            grid=(row_count // TILE,),
            in_specs=in_specs,
            out_specs=pl.BlockSpec((TILE, out_cols, out_width), lambda t, s: (t, 0, 0)),
        ),
        out_shape=jax.ShapeDtypeStruct(
            (row_count, out_cols, out_width), jnp.bfloat16 if final else jnp.float32
        ),
        compiler_params=pltpu.CompilerParams(vmem_limit_bytes=40 * 1024 * 1024),
        cost_estimate=pl.CostEstimate(flops=1024, bytes_accessed=1024, transcendentals=0),
    )(scalars, *operands)


def by_member(filters, first, count):
    _, across, shard, out_local = filters.shape
    split = out_local // GROUP
    if split % 128:
        taps = filters[first : first + count].reshape(count * across, shard, out_local)
        return jnp.stack([taps[..., r * split : (r + 1) * split] for r in range(GROUP)])

    def body(taps, out):
        for r in range(GROUP):
            out[r, 0] = taps[0, 0, :, r * split : (r + 1) * split]

    return pl.pallas_call(
        body,
        grid=(count, across),
        in_specs=[pl.BlockSpec((1, 1, shard, out_local), lambda v, b: (first + v, b, 0, 0))],
        out_specs=pl.BlockSpec(
            (GROUP, 1, shard, split), lambda v, b: (0, v * across + b, 0, 0)
        ),
        out_shape=jax.ShapeDtypeStruct((GROUP, count * across, shard, split), filters.dtype),
    )(filters)


def local(activations, filters, channel_bias):
    rows, side, depth = activations.shape
    shard, out_local = filters.shape[2:]
    size, chans = lax.axis_size("img"), lax.axis_size("ch")
    me, mine = lax.axis_index("img"), lax.axis_index("ch")
    parts = size // GROUP
    group, rank = me // GROUP, me % GROUP
    members = [[g * GROUP + r for r in range(GROUP)] for g in range(parts)]
    split = out_local // GROUP

    def share(taps):
        return lax.all_to_all(taps, "img", 0, 0, axis_index_groups=members, tiled=True)

    def exchange(array):
        return [swap(array, "img", GROUP * j) for j in range(1, parts)]

    ready = []

    def step(array):
        return after(array, *ready) if ready else array

    first, activations = lax.optimization_barrier((filters[0, :1], activations))
    taken = [exchange(first)]
    taken.append(exchange(after(filters[0, 1:2], *taken[0])))

    ups = [(i, i + 1) for i in range(size - 1)]
    above = lax.ppermute(activations[-1:], "img", ups)
    below = lax.ppermute(activations[:1], "img", [(j, i) for i, j in ups])
    piece = jnp.where(
        rank >= GROUP // 2,
        jnp.concatenate([activations, below], axis=0),
        jnp.concatenate([above, activations], axis=0),
    )
    slots = {(0, 0): piece}
    width = -(-side // 16) * 16
    image = jnp.zeros((chans, GROUP * rows + 3, width, depth), activations.dtype)

    def over_ch(r):
        sent = step(slots[0, r])
        for j in range(1, chans):
            slots[j, r] = swap(sent, "ch", j)

    def over_core(keys):
        for j, r in keys:
            slots[j, r + 1] = swap(step(slots[j, r]), "img", 1)

    def place(image, keys):
        for j, r in keys:
            owner = rank ^ r
            start = owner * rows + (owner >= GROUP // 2).astype(jnp.int32)
            image = lax.dynamic_update_slice(image, slots[j, r][None], (mine ^ j, start, 0, 0))
        return image

    others = range(1, chans)

    by_rank = by_member(filters, 1, 2)
    over_ch(0)
    slots[0, 4] = swap(piece, "img", 4)
    slots[0, 2] = swap(piece, "img", 2)
    ready = [*taken[1], slots[0, 4], slots[0, 2], *(slots[j, 0] for j in others), by_rank]

    lower = share(step(by_rank))
    over_ch(4)
    over_ch(2)
    slots[0, 6] = swap(step(slots[0, 4]), "img", 2)
    taken.append(exchange(step(filters[0, 2:])))
    ready = [lower, *taken[2], slots[0, 6], *(slots[j, r] for j in others for r in (4, 2))]

    half = GROUP // 2
    received = [exchange(step(lower[:half]))]
    over_ch(6)
    raw = [filters[0]] + [
        jnp.concatenate([step(array) for array in arrays]) for arrays in zip(*taken)
    ]
    upper = share(by_member(jnp.stack(raw), 0, parts))
    late = [(j, 6) for j in others]
    keys = [key for key in slots if key not in late]
    over_core(keys)
    image = place(image, keys + [(j, r + 1) for j, r in keys])
    ready = []
    over_core(late)
    image = place(image, late + [(j, r + 1) for j, r in late])

    scalars = jnp.stack([group * GROUP * rows, group]).astype(jnp.int32)
    bias = lax.dynamic_slice_in_dim(channel_bias, rank * split, split)[None]
    which = [lambda s, j=j: s[1] ^ j for j in range(parts)]

    at_start = lambda s: (0, 0, 0, 0)

    def pieces(start, arrays):
        return [
            (which[j], start, array, array.shape, at_start, (1, 2))
            for j, array in enumerate(arrays, 1)
        ]

    every = [
        (which[j], 0, upper, (GROUP, 3, shard, split), lambda s, j=j: (0, j, 0, 0), (0,))
        for j in range(parts)
    ]
    own = [(which[0], 0, lower, lower.shape, at_start, (1, 2))]
    acc = conv_call(own, scalars, image)
    received.append(exchange(after(lower[half:], *received[0], acc, upper)))
    acc = conv_call(every + pieces(0, received[0]), scalars, image, acc)
    out = conv_call(pieces(half, received[1]), scalars, image, acc, bias)
    out = share(out).reshape(GROUP, rows, side, split)
    return jnp.moveaxis(out, 0, 2).reshape(rows, side, out_local)


def solution(mesh):
    placed = (P("img", None, "ch"), P(None, None, "img", "ch"), P("ch"))
    return jax.shard_map(
        local, mesh=mesh, in_specs=placed, out_specs=P("img", None, "ch"), check_vma=False
    )
```

```python
import jax
import jax.numpy as jnp
from jax import lax
from jax.experimental import pallas as pl
from jax.experimental.pallas import tpu as pltpu
from jax.sharding import PartitionSpec as P

SIDE = 56
GROUP = 8
TILE = 8


def swap(array, axis, bit):
    size = lax.axis_size(axis)
    return lax.ppermute(array, axis, [(i, i ^ bit) for i in range(size)])


def after(array, *others):
    return lax.optimization_barrier((array, *others))[0]


def conv_call(pieces, scalars, image, acc=None, bias=None):
    blocks, padded_rows, width, depth = image.shape
    shard, out_width = pieces[0][3][-2:]
    row_count = padded_rows - 3
    offsets = list(dict.fromkeys(piece[0] for piece in pieces))
    per_group = GROUP * shard // depth
    final = bias is not None
    assert row_count % TILE == 0 and SIDE % TILE == 0

    edges_of = {
        offset: sorted({v for o, *_, taps in pieces if o == offset for v in taps if v != 1})
        for offset in offsets
    }
    windows = {}
    for offset in offsets:
        ranges = [(start, start + block[-4]) for o, start, _, block, *_ in pieces if o == offset]
        low, high = min(a for a, _ in ranges) * shard, max(b for _, b in ranges) * shard
        if low // depth == (high - 1) // depth:
            windows[offset] = (1, low // depth, high - low, low % depth)
        else:
            windows[offset] = (per_group, 0, depth, 0)

    def body(scalars_ref, *refs):
        refs = list(refs)
        images = {}
        for offset in offsets:
            images[offset] = refs.pop(0), {v: refs.pop(0) for v in edges_of[offset]}
        weights = [refs.pop(0) for _ in pieces]
        acc_ref = refs.pop(0) if acc is not None else None
        bias_ref = refs.pop(0) if final else None
        out = refs.pop(0)

        operands, columns = [], []
        for (offset, start, _, block, _, taps), weight in zip(pieces, weights):
            count, first_block, size, first_lane = windows[offset]
            main, edges = images[offset]
            at, lanes = 0, block[-4] * shard
            while at < lanes:
                inner, lane = divmod(start * shard + at, depth)
                inner, lane = inner - first_block, lane - first_lane
                length = min(size - lane, lanes - at)
                window = pl.ds(lane, length)
                for index, vertical in enumerate(taps):
                    rows = main[inner, :, :, window]
                    if vertical == 0:
                        rows = jnp.concatenate(
                            [edges[0][inner, :, :, window], rows[:-1]], axis=0
                        )
                    if vertical == 2:
                        rows = jnp.concatenate(
                            [rows[1:], edges[2][inner, :, :, window]], axis=0
                        )
                    operands.append(rows.reshape(TILE * width, length))
                    members = pl.ds(at // shard, length // shard)
                    columns.append(
                        [
                            weight[members, 3 * index + b].reshape(length, out_width)
                            for b in range(3)
                        ]
                    )
                at += length
        operand = jnp.concatenate(operands, axis=1)
        total = None
        for horizontal in range(3):
            value = jnp.dot(
                operand,
                jnp.concatenate([c[horizontal] for c in columns], axis=0),
                preferred_element_type=jnp.float32,
            ).reshape(TILE, width, out_width)
            if horizontal != 1:
                value = pltpu.roll(value, (1 - horizontal) % width, 1)
            total = value if total is None else total + value
        if acc_ref is not None:
            total = total + acc_ref[...]
        if final:
            total = (total + bias_ref[...].reshape(1, 1, -1))[:, : out.shape[1]]
        out[...] = total.astype(out.dtype)

    def image_spec(offset, vertical):
        count, first_block, size, first_lane = windows[offset]
        rows = TILE if vertical == 1 else 1

        def place(t, s):
            row = t * TILE + 1
            if vertical == 0:
                row = jnp.where((s[0] + t * TILE) % SIDE == 0, row_count + 2, row - 1)
            if vertical == 2:
                row = jnp.where((s[0] + (t + 1) * TILE) % SIDE == 0, row_count + 2, row + TILE)
            return (offset(s) * per_group + first_block, row, 0, first_lane)

        return pl.BlockSpec(tuple(pl.Element(n) for n in (count, rows, width, size)), place)

    out_cols = SIDE if final else width
    in_specs, operands = [], []
    for offset in offsets:
        for vertical in [1] + edges_of[offset]:
            in_specs.append(image_spec(offset, vertical))
            operands.append(image)
    for _, _, array, block, place, _ in pieces:
        in_specs.append(pl.BlockSpec(block, lambda t, s, place=place: place(s)))
        operands.append(array)
    if acc is not None:
        in_specs.append(pl.BlockSpec((TILE, width, out_width), lambda t, s: (t, 0, 0)))
        operands.append(acc)
    if final:
        in_specs.append(pl.BlockSpec((1, out_width), lambda t, s: (0, 0)))
        operands.append(bias)
    return pl.pallas_call(
        body,
        grid_spec=pltpu.PrefetchScalarGridSpec(
            num_scalar_prefetch=1,
            grid=(row_count // TILE,),
            in_specs=in_specs,
            out_specs=pl.BlockSpec((TILE, out_cols, out_width), lambda t, s: (t, 0, 0)),
        ),
        out_shape=jax.ShapeDtypeStruct(
            (row_count, out_cols, out_width), jnp.bfloat16 if final else jnp.float32
        ),
        compiler_params=pltpu.CompilerParams(vmem_limit_bytes=40 * 1024 * 1024),
        cost_estimate=pl.CostEstimate(flops=1024, bytes_accessed=1024, transcendentals=0),
    )(scalars, *operands)


def by_member(filters, first, count):
    _, across, shard, out_local = filters.shape
    split = out_local // GROUP
    if split % 128:
        taps = filters[first : first + count].reshape(count * across, shard, out_local)
        return jnp.stack([taps[..., r * split : (r + 1) * split] for r in range(GROUP)])

    def body(taps, out):
        for r in range(GROUP):
            out[r, 0] = taps[0, 0, :, r * split : (r + 1) * split]

    return pl.pallas_call(
        body,
        grid=(count, across),
        in_specs=[pl.BlockSpec((1, 1, shard, out_local), lambda v, b: (first + v, b, 0, 0))],
        out_specs=pl.BlockSpec(
            (GROUP, 1, shard, split), lambda v, b: (0, v * across + b, 0, 0)
        ),
        out_shape=jax.ShapeDtypeStruct((GROUP, count * across, shard, split), filters.dtype),
    )(filters)


def local(activations, filters, channel_bias):
    rows, side, depth = activations.shape
    shard, out_local = filters.shape[2:]
    size, chans = lax.axis_size("img"), lax.axis_size("ch")
    me, mine = lax.axis_index("img"), lax.axis_index("ch")
    parts = size // GROUP
    group, rank = me // GROUP, me % GROUP
    members = [[g * GROUP + r for r in range(GROUP)] for g in range(parts)]
    split = out_local // GROUP

    def share(taps):
        return lax.all_to_all(taps, "img", 0, 0, axis_index_groups=members, tiled=True)

    def exchange(array):
        return [swap(array, "img", GROUP * j) for j in range(1, parts)]

    ready = []

    def step(array):
        return after(array, *ready) if ready else array

    first, activations = lax.optimization_barrier((filters[0, :2], activations))
    second = filters[0, 2:]
    ups = [(i, i + 1) for i in range(size - 1)]
    above = lax.ppermute(activations[-1:], "img", ups)
    below = lax.ppermute(activations[:1], "img", [(j, i) for i, j in ups])
    piece = jnp.where(
        rank >= GROUP // 2,
        jnp.concatenate([activations, below], axis=0),
        jnp.concatenate([above, activations], axis=0),
    )
    slots = {(0, 0): piece}
    width = -(-side // 16) * 16
    image = jnp.zeros((chans, GROUP * rows + 3, width, depth), activations.dtype)

    def over_ch(r):
        sent = step(slots[0, r])
        for j in range(1, chans):
            slots[j, r] = swap(sent, "ch", j)

    def over_core(keys):
        for j, r in keys:
            slots[j, r + 1] = swap(step(slots[j, r]), "img", 1)

    def place(image, keys):
        for j, r in keys:
            owner = rank ^ r
            start = owner * rows + (owner >= GROUP // 2).astype(jnp.int32)
            image = lax.dynamic_update_slice(image, slots[j, r][None], (mine ^ j, start, 0, 0))
        return image

    others = range(1, chans)

    taken = exchange(first)
    by_rank = by_member(filters, 1, 2)
    over_ch(0)
    slots[0, 4] = swap(piece, "img", 4)
    slots[0, 2] = swap(piece, "img", 2)
    ready = [*taken, slots[0, 4], slots[0, 2], *(slots[j, 0] for j in others), by_rank]

    lower = share(step(by_rank))
    over_ch(4)
    taken_last = exchange(step(second))
    keys = [(0, 0), (0, 4), (0, 2)] + [(j, 0) for j in others]
    over_core(keys)
    image = place(image, keys)
    ready = [lower, *(slots[j, 4] for j in others), *taken_last]
    ready += [slots[j, r + 1] for j, r in keys]

    received = exchange(step(lower))
    over_ch(2)
    slots[0, 6] = swap(step(slots[0, 4]), "img", 2)
    image = place(image, [(j, r + 1) for j, r in keys])
    raw = [filters[0]] + [
        jnp.concatenate([step(a), step(b)]) for a, b in zip(taken, taken_last)
    ]
    upper = share(by_member(jnp.stack(raw), 0, parts))
    ready = []
    over_ch(6)
    keys = [(0, 6)] + [(j, r) for r in (4, 2, 6) for j in others]
    over_core(keys)
    image = place(image, keys + [(j, r + 1) for j, r in keys])

    scalars = jnp.stack([group * GROUP * rows, group]).astype(jnp.int32)
    bias = lax.dynamic_slice_in_dim(channel_bias, rank * split, split)[None]
    which = [lambda s, j=j: s[1] ^ j for j in range(parts)]
    at_start = lambda s: (0, 0, 0, 0)
    blocks = [(which[j], 0, array, array.shape, at_start, (1, 2))
              for j, array in enumerate([lower, *received])]
    every = [
        (which[j], 0, upper, (GROUP, 3, shard, split), lambda s, j=j: (0, j, 0, 0), (0,))
        for j in range(parts)
    ]
    acc = conv_call(blocks[:1], scalars, image)
    acc = conv_call(every, scalars, image, acc)
    out = conv_call(blocks[1:], scalars, image, acc, bias)
    out = share(out).reshape(GROUP, rows, side, split)
    return jnp.moveaxis(out, 0, 2).reshape(rows, side, out_local)


def solution(mesh):
    placed = (P("img", None, "ch"), P(None, None, "img", "ch"), P("ch"))
    return jax.shard_map(
        local, mesh=mesh, in_specs=placed, out_specs=P("img", None, "ch"), check_vma=False
    )
```

```python
import jax
import jax.numpy as jnp
from jax import lax
from jax.experimental import pallas as pl
from jax.experimental.pallas import tpu as pltpu
from jax.sharding import PartitionSpec as P

SIDE = 56
GROUP = 8
TILE = 8


def swap(array, axis, bit):
    size = lax.axis_size(axis)
    return lax.ppermute(array, axis, [(i, i ^ bit) for i in range(size)])


def after(array, *others):
    return lax.optimization_barrier((array, *others))[0]


def conv_call(pieces, scalars, image, acc=None, bias=None):
    blocks, padded_rows, width, depth = image.shape
    shard, out_width = pieces[0][3][-2:]
    row_count = padded_rows - 3
    offsets = list(dict.fromkeys(piece[0] for piece in pieces))
    per_group = GROUP * shard // depth
    final = bias is not None
    assert row_count % TILE == 0 and SIDE % TILE == 0

    edges_of = {
        offset: sorted({v for o, *_, taps in pieces if o == offset for v in taps if v != 1})
        for offset in offsets
    }
    windows = {}
    for offset in offsets:
        ranges = [(start, start + block[-4]) for o, start, _, block, *_ in pieces if o == offset]
        low, high = min(a for a, _ in ranges) * shard, max(b for _, b in ranges) * shard
        if low // depth == (high - 1) // depth:
            windows[offset] = (1, low // depth, high - low, low % depth)
        else:
            windows[offset] = (per_group, 0, depth, 0)

    def body(scalars_ref, *refs):
        refs = list(refs)
        images = {}
        for offset in offsets:
            images[offset] = refs.pop(0), {v: refs.pop(0) for v in edges_of[offset]}
        weights = [refs.pop(0) for _ in pieces]
        acc_ref = refs.pop(0) if acc is not None else None
        bias_ref = refs.pop(0) if final else None
        out = refs.pop(0)

        operands, columns = [], []
        for (offset, start, _, block, _, taps), weight in zip(pieces, weights):
            count, first_block, size, first_lane = windows[offset]
            main, edges = images[offset]
            at, lanes = 0, block[-4] * shard
            while at < lanes:
                inner, lane = divmod(start * shard + at, depth)
                inner, lane = inner - first_block, lane - first_lane
                length = min(size - lane, lanes - at)
                window = pl.ds(lane, length)
                for index, vertical in enumerate(taps):
                    rows = main[inner, :, :, window]
                    if vertical == 0:
                        rows = jnp.concatenate(
                            [edges[0][inner, :, :, window], rows[:-1]], axis=0
                        )
                    if vertical == 2:
                        rows = jnp.concatenate(
                            [rows[1:], edges[2][inner, :, :, window]], axis=0
                        )
                    operands.append(rows.reshape(TILE * width, length))
                    members = pl.ds(at // shard, length // shard)
                    columns.append(
                        [
                            weight[members, 3 * index + b].reshape(length, out_width)
                            for b in range(3)
                        ]
                    )
                at += length
        operand = jnp.concatenate(operands, axis=1)
        total = None
        for horizontal in range(3):
            value = jnp.dot(
                operand,
                jnp.concatenate([c[horizontal] for c in columns], axis=0),
                preferred_element_type=jnp.float32,
            ).reshape(TILE, width, out_width)
            if horizontal != 1:
                value = pltpu.roll(value, (1 - horizontal) % width, 1)
            total = value if total is None else total + value
        if acc_ref is not None:
            total = total + acc_ref[...]
        if final:
            total = (total + bias_ref[...].reshape(1, 1, -1))[:, : out.shape[1]]
        out[...] = total.astype(out.dtype)

    def image_spec(offset, vertical):
        count, first_block, size, first_lane = windows[offset]
        rows = TILE if vertical == 1 else 1

        def place(t, s):
            row = t * TILE + 1
            if vertical == 0:
                row = jnp.where((s[0] + t * TILE) % SIDE == 0, row_count + 2, row - 1)
            if vertical == 2:
                row = jnp.where((s[0] + (t + 1) * TILE) % SIDE == 0, row_count + 2, row + TILE)
            return (offset(s) * per_group + first_block, row, 0, first_lane)

        return pl.BlockSpec(tuple(pl.Element(n) for n in (count, rows, width, size)), place)

    out_cols = SIDE if final else width
    in_specs, operands = [], []
    for offset in offsets:
        for vertical in [1] + edges_of[offset]:
            in_specs.append(image_spec(offset, vertical))
            operands.append(image)
    for _, _, array, block, place, _ in pieces:
        in_specs.append(pl.BlockSpec(block, lambda t, s, place=place: place(s)))
        operands.append(array)
    if acc is not None:
        in_specs.append(pl.BlockSpec((TILE, width, out_width), lambda t, s: (t, 0, 0)))
        operands.append(acc)
    if final:
        in_specs.append(pl.BlockSpec((1, out_width), lambda t, s: (0, 0)))
        operands.append(bias)
    return pl.pallas_call(
        body,
        grid_spec=pltpu.PrefetchScalarGridSpec(
            num_scalar_prefetch=1,
            grid=(row_count // TILE,),
            in_specs=in_specs,
            out_specs=pl.BlockSpec((TILE, out_cols, out_width), lambda t, s: (t, 0, 0)),
        ),
        out_shape=jax.ShapeDtypeStruct(
            (row_count, out_cols, out_width), jnp.bfloat16 if final else jnp.float32
        ),
        compiler_params=pltpu.CompilerParams(vmem_limit_bytes=40 * 1024 * 1024),
        cost_estimate=pl.CostEstimate(flops=1024, bytes_accessed=1024, transcendentals=0),
    )(scalars, *operands)


def by_member(filters, first, count):
    _, across, shard, out_local = filters.shape
    split = out_local // GROUP
    if split % 128:
        taps = filters[first : first + count].reshape(count * across, shard, out_local)
        return jnp.stack([taps[..., r * split : (r + 1) * split] for r in range(GROUP)])

    def body(taps, out):
        for r in range(GROUP):
            out[r, 0] = taps[0, 0, :, r * split : (r + 1) * split]

    return pl.pallas_call(
        body,
        grid=(count, across),
        in_specs=[pl.BlockSpec((1, 1, shard, out_local), lambda v, b: (first + v, b, 0, 0))],
        out_specs=pl.BlockSpec(
            (GROUP, 1, shard, split), lambda v, b: (0, v * across + b, 0, 0)
        ),
        out_shape=jax.ShapeDtypeStruct((GROUP, count * across, shard, split), filters.dtype),
    )(filters)


def local(activations, filters, channel_bias):
    rows, side, depth = activations.shape
    shard, out_local = filters.shape[2:]
    size, chans = lax.axis_size("img"), lax.axis_size("ch")
    me, mine = lax.axis_index("img"), lax.axis_index("ch")
    parts = size // GROUP
    group, rank = me // GROUP, me % GROUP
    members = [[g * GROUP + r for r in range(GROUP)] for g in range(parts)]
    split = out_local // GROUP

    def share(taps):
        return lax.all_to_all(taps, "img", 0, 0, axis_index_groups=members, tiled=True)

    def exchange(array):
        return [swap(array, "img", GROUP * j) for j in range(1, parts)]

    ready = []

    def step(array):
        return after(array, *ready) if ready else array

    first, activations = lax.optimization_barrier((filters[0, :2], activations))
    second = filters[0, 2:]
    ups = [(i, i + 1) for i in range(size - 1)]
    above = lax.ppermute(activations[-1:], "img", ups)
    below = lax.ppermute(activations[:1], "img", [(j, i) for i, j in ups])
    piece = jnp.where(
        rank >= GROUP // 2,
        jnp.concatenate([activations, below], axis=0),
        jnp.concatenate([above, activations], axis=0),
    )
    slots = {(0, 0): piece}
    width = -(-side // 16) * 16
    image = jnp.zeros((chans, GROUP * rows + 3, width, depth), activations.dtype)

    def over_ch(r):
        sent = step(slots[0, r])
        for j in range(1, chans):
            slots[j, r] = swap(sent, "ch", j)

    def over_core(keys):
        for j, r in keys:
            slots[j, r + 1] = swap(step(slots[j, r]), "img", 1)

    def place(image, keys):
        for j, r in keys:
            owner = rank ^ r
            start = owner * rows + (owner >= GROUP // 2).astype(jnp.int32)
            image = lax.dynamic_update_slice(image, slots[j, r][None], (mine ^ j, start, 0, 0))
        return image

    others = range(1, chans)

    taken = exchange(first)
    by_rank = by_member(filters, 1, 2)
    over_ch(0)
    slots[0, 4] = swap(piece, "img", 4)
    slots[0, 2] = swap(piece, "img", 2)
    ready = [*taken, slots[0, 4], slots[0, 2], *(slots[j, 0] for j in others), by_rank]

    lower = share(step(by_rank))
    over_ch(4)
    taken_last = exchange(step(second))
    keys = [(0, 0), (0, 4), (0, 2)] + [(j, 0) for j in others]
    over_core(keys)
    image = place(image, keys)
    ready = [lower, *(slots[j, 4] for j in others), *taken_last]
    ready += [slots[j, r + 1] for j, r in keys]

    cuts = (0, GROUP // 4, GROUP - GROUP // 4, GROUP)
    chunks = [lower[a:b] for a, b in zip(cuts, cuts[1:])]
    received = [exchange(step(chunks[0]))]
    over_ch(2)
    slots[0, 6] = swap(step(slots[0, 4]), "img", 2)
    image = place(image, [(j, r + 1) for j, r in keys])
    keys = [(j, 4) for j in others]
    over_core(keys)
    image = place(image, keys)
    raw = [filters[0]] + [
        jnp.concatenate([step(a), step(b)]) for a, b in zip(taken, taken_last)
    ]
    by_rank = by_member(jnp.stack(raw), 0, parts)
    ready = [*received[0], slots[0, 6], *(slots[j, 2] for j in others), image, by_rank]
    ready += [slots[j, r + 1] for j, r in keys]

    received.append(exchange(step(chunks[1])))
    over_ch(6)
    upper = share(step(by_rank))
    image = place(image, [(j, r + 1) for j, r in keys])
    keys = [(0, 6)] + [(j, 2) for j in others]
    over_core(keys)
    image = place(image, keys)
    image = place(image, [(j, r + 1) for j, r in keys])
    ready = []
    keys = [(j, 6) for j in others]
    over_core(keys)
    image = place(image, keys)
    image = place(image, [(j, r + 1) for j, r in keys])

    scalars = jnp.stack([group * GROUP * rows, group]).astype(jnp.int32)
    bias = lax.dynamic_slice_in_dim(channel_bias, rank * split, split)[None]
    which = [lambda s, j=j: s[1] ^ j for j in range(parts)]
    at_start = lambda s: (0, 0, 0, 0)
    every = [
        (which[j], 0, upper, (GROUP, 3, shard, split), lambda s, j=j: (0, j, 0, 0), (0,))
        for j in range(parts)
    ]

    def pieces(chosen):
        return [
            (which[j], cuts[c], array, array.shape, at_start, (1, 2))
            for c in chosen
            for j, array in enumerate(received[c], 1)
        ]

    acc = conv_call([(which[0], 0, lower, lower.shape, at_start, (1, 2))], scalars, image)
    received.append(exchange(after(chunks[2], *received[1], acc, upper)))
    acc = conv_call(every + pieces((0, 1)), scalars, image, acc)
    out = conv_call(pieces((2,)), scalars, image, acc, bias)
    out = share(out).reshape(GROUP, rows, side, split)
    return jnp.moveaxis(out, 0, 2).reshape(rows, side, out_local)


def solution(mesh):
    placed = (P("img", None, "ch"), P(None, None, "img", "ch"), P("ch"))
    return jax.shard_map(
        local, mesh=mesh, in_specs=placed, out_specs=P("img", None, "ch"), check_vma=False
    )
```

```python
import jax
import jax.numpy as jnp
from jax import lax
from jax.experimental import pallas as pl
from jax.experimental.pallas import tpu as pltpu
from jax.sharding import PartitionSpec as P

SIDE = 56
GROUP = 8
TILE = 8


def swap(array, axis, bit):
    size = lax.axis_size(axis)
    return lax.ppermute(array, axis, [(i, i ^ bit) for i in range(size)])


def after(array, *others):
    return lax.optimization_barrier((array, *others))[0]


def conv_call(pieces, scalars, image, acc=None, bias=None):
    blocks, padded_rows, width, depth = image.shape
    shard, out_width = pieces[0][3][-2:]
    row_count = padded_rows - 3
    offsets = list(dict.fromkeys(piece[0] for piece in pieces))
    per_group = GROUP * shard // depth
    final = bias is not None
    assert row_count % TILE == 0 and SIDE % TILE == 0

    edges_of = {
        offset: sorted({v for o, *_, taps in pieces if o == offset for v in taps if v != 1})
        for offset in offsets
    }
    windows = {}
    for offset in offsets:
        ranges = [(start, start + block[-4]) for o, start, _, block, *_ in pieces if o == offset]
        low, high = min(a for a, _ in ranges) * shard, max(b for _, b in ranges) * shard
        if low // depth == (high - 1) // depth:
            windows[offset] = (1, low // depth, high - low, low % depth)
        else:
            windows[offset] = (per_group, 0, depth, 0)

    def body(scalars_ref, *refs):
        refs = list(refs)
        images = {}
        for offset in offsets:
            images[offset] = refs.pop(0), {v: refs.pop(0) for v in edges_of[offset]}
        weights = [refs.pop(0) for _ in pieces]
        acc_ref = refs.pop(0) if acc is not None else None
        bias_ref = refs.pop(0) if final else None
        out = refs.pop(0)

        operands, columns = [], []
        for (offset, start, _, block, _, taps), weight in zip(pieces, weights):
            count, first_block, size, first_lane = windows[offset]
            main, edges = images[offset]
            at, lanes = 0, block[-4] * shard
            while at < lanes:
                inner, lane = divmod(start * shard + at, depth)
                inner, lane = inner - first_block, lane - first_lane
                length = min(size - lane, lanes - at)
                window = pl.ds(lane, length)
                for index, vertical in enumerate(taps):
                    rows = main[inner, :, :, window]
                    if vertical == 0:
                        rows = jnp.concatenate(
                            [edges[0][inner, :, :, window], rows[:-1]], axis=0
                        )
                    if vertical == 2:
                        rows = jnp.concatenate(
                            [rows[1:], edges[2][inner, :, :, window]], axis=0
                        )
                    operands.append(rows.reshape(TILE * width, length))
                    members = pl.ds(at // shard, length // shard)
                    columns.append(
                        [
                            weight[members, 3 * index + b].reshape(length, out_width)
                            for b in range(3)
                        ]
                    )
                at += length
        operand = jnp.concatenate(operands, axis=1)
        total = None
        for horizontal in range(3):
            value = jnp.dot(
                operand,
                jnp.concatenate([c[horizontal] for c in columns], axis=0),
                preferred_element_type=jnp.float32,
            ).reshape(TILE, width, out_width)
            if horizontal != 1:
                value = pltpu.roll(value, (1 - horizontal) % width, 1)
            total = value if total is None else total + value
        if acc_ref is not None:
            total = total + acc_ref[...]
        if final:
            total = (total + bias_ref[...].reshape(1, 1, -1))[:, : out.shape[1]]
        out[...] = total.astype(out.dtype)

    def image_spec(offset, vertical):
        count, first_block, size, first_lane = windows[offset]
        rows = TILE if vertical == 1 else 1

        def place(t, s):
            row = t * TILE + 1
            if vertical == 0:
                row = jnp.where((s[0] + t * TILE) % SIDE == 0, row_count + 2, row - 1)
            if vertical == 2:
                row = jnp.where((s[0] + (t + 1) * TILE) % SIDE == 0, row_count + 2, row + TILE)
            return (offset(s) * per_group + first_block, row, 0, first_lane)

        return pl.BlockSpec(tuple(pl.Element(n) for n in (count, rows, width, size)), place)

    out_cols = SIDE if final else width
    in_specs, operands = [], []
    for offset in offsets:
        for vertical in [1] + edges_of[offset]:
            in_specs.append(image_spec(offset, vertical))
            operands.append(image)
    for _, _, array, block, place, _ in pieces:
        in_specs.append(pl.BlockSpec(block, lambda t, s, place=place: place(s)))
        operands.append(array)
    if acc is not None:
        in_specs.append(pl.BlockSpec((TILE, width, out_width), lambda t, s: (t, 0, 0)))
        operands.append(acc)
    if final:
        in_specs.append(pl.BlockSpec((1, out_width), lambda t, s: (0, 0)))
        operands.append(bias)
    return pl.pallas_call(
        body,
        grid_spec=pltpu.PrefetchScalarGridSpec(
            num_scalar_prefetch=1,
            grid=(row_count // TILE,),
            in_specs=in_specs,
            out_specs=pl.BlockSpec((TILE, out_cols, out_width), lambda t, s: (t, 0, 0)),
        ),
        out_shape=jax.ShapeDtypeStruct(
            (row_count, out_cols, out_width), jnp.bfloat16 if final else jnp.float32
        ),
        compiler_params=pltpu.CompilerParams(vmem_limit_bytes=40 * 1024 * 1024),
        cost_estimate=pl.CostEstimate(flops=1024, bytes_accessed=1024, transcendentals=0),
    )(scalars, *operands)


def by_member(filters, first, count):
    _, across, shard, out_local = filters.shape
    split = out_local // GROUP
    if split % 128:
        taps = filters[first : first + count].reshape(count * across, shard, out_local)
        return jnp.stack([taps[..., r * split : (r + 1) * split] for r in range(GROUP)])

    def body(taps, out):
        for r in range(GROUP):
            out[r, 0] = taps[0, 0, :, r * split : (r + 1) * split]

    return pl.pallas_call(
        body,
        grid=(count, across),
        in_specs=[pl.BlockSpec((1, 1, shard, out_local), lambda v, b: (first + v, b, 0, 0))],
        out_specs=pl.BlockSpec(
            (GROUP, 1, shard, split), lambda v, b: (0, v * across + b, 0, 0)
        ),
        out_shape=jax.ShapeDtypeStruct((GROUP, count * across, shard, split), filters.dtype),
    )(filters)


def local(activations, filters, channel_bias):
    rows, side, depth = activations.shape
    shard, out_local = filters.shape[2:]
    size, chans = lax.axis_size("img"), lax.axis_size("ch")
    me, mine = lax.axis_index("img"), lax.axis_index("ch")
    parts = size // GROUP
    group, rank = me // GROUP, me % GROUP
    members = [[g * GROUP + r for r in range(GROUP)] for g in range(parts)]
    split = out_local // GROUP

    def share(taps):
        return lax.all_to_all(taps, "img", 0, 0, axis_index_groups=members, tiled=True)

    def exchange(array):
        return [swap(array, "img", GROUP * j) for j in range(1, parts)]

    ready = []

    def step(array):
        return after(array, *ready) if ready else array

    first, activations = lax.optimization_barrier((filters[0, :2], activations))
    second = filters[0, 2:]
    ups = [(i, i + 1) for i in range(size - 1)]
    above = lax.ppermute(activations[-1:], "img", ups)
    below = lax.ppermute(activations[:1], "img", [(j, i) for i, j in ups])
    piece = jnp.where(
        rank >= GROUP // 2,
        jnp.concatenate([activations, below], axis=0),
        jnp.concatenate([above, activations], axis=0),
    )
    slots = {(0, 0): piece}
    width = -(-side // 16) * 16
    image = jnp.zeros((chans, GROUP * rows + 3, width, depth), activations.dtype)

    def over_ch(r):
        sent = step(slots[0, r])
        for j in range(1, chans):
            slots[j, r] = swap(sent, "ch", j)

    def over_core(keys):
        for j, r in keys:
            slots[j, r + 1] = swap(step(slots[j, r]), "img", 1)

    def place(image, keys):
        for j, r in keys:
            owner = rank ^ r
            start = owner * rows + (owner >= GROUP // 2).astype(jnp.int32)
            image = lax.dynamic_update_slice(image, slots[j, r][None], (mine ^ j, start, 0, 0))
        return image

    others = range(1, chans)

    taken = exchange(first)
    by_rank = by_member(filters, 1, 2)
    over_ch(0)
    slots[0, 4] = swap(piece, "img", 4)
    slots[0, 2] = swap(piece, "img", 2)
    ready = [*taken, slots[0, 4], slots[0, 2], *(slots[j, 0] for j in others), by_rank]

    lower = share(step(by_rank))
    over_ch(4)
    taken_last = exchange(step(second))
    keys = [(0, 0), (0, 4), (0, 2)] + [(j, 0) for j in others]
    over_core(keys)
    image = place(image, keys)
    ready = [lower, *(slots[j, 4] for j in others), *taken_last]
    ready += [slots[j, r + 1] for j, r in keys]

    cuts = (0, GROUP // 4, GROUP - GROUP // 4, GROUP)
    chunks = [lower[a:b] for a, b in zip(cuts, cuts[1:])]
    received = [exchange(step(chunks[0]))]
    over_ch(2)
    slots[0, 6] = swap(step(slots[0, 4]), "img", 2)
    image = place(image, [(j, r + 1) for j, r in keys])
    keys = [(j, 4) for j in others]
    over_core(keys)
    image = place(image, keys)
    raw = [filters[0]] + [
        jnp.concatenate([step(a), step(b)]) for a, b in zip(taken, taken_last)
    ]
    by_rank = by_member(jnp.stack(raw), 0, parts)
    ready = [slots[0, 6], *(slots[j, 2] for j in others), image, by_rank]
    ready += [slots[j, r + 1] for j, r in keys]

    received.append(exchange(after(chunks[1], *ready, *received[0])))
    over_ch(6)
    upper = share(step(by_rank))
    image = place(image, [(j, r + 1) for j, r in keys])
    keys = [(0, 6)] + [(j, 2) for j in others]
    over_core(keys)
    image = place(image, keys)
    image = place(image, [(j, r + 1) for j, r in keys])
    ready = []
    keys = [(j, 6) for j in others]
    over_core(keys)
    image = place(image, keys)
    image = place(image, [(j, r + 1) for j, r in keys])

    scalars = jnp.stack([group * GROUP * rows, group]).astype(jnp.int32)
    bias = lax.dynamic_slice_in_dim(channel_bias, rank * split, split)[None]
    which = [lambda s, j=j: s[1] ^ j for j in range(parts)]
    at_start = lambda s: (0, 0, 0, 0)
    every = [
        (which[j], 0, upper, (GROUP, 3, shard, split), lambda s, j=j: (0, j, 0, 0), (0,))
        for j in range(parts)
    ]

    def pieces(chosen):
        return [
            (which[j], cuts[c], array, array.shape, at_start, (1, 2))
            for c in chosen
            for j, array in enumerate(received[c], 1)
        ]

    acc = conv_call([(which[0], 0, lower, lower.shape, at_start, (1, 2))], scalars, image)
    received.append(exchange(after(chunks[2], *received[1], acc, upper)))
    acc = conv_call(every + pieces((0, 1)), scalars, image, acc)
    out = conv_call(pieces((2,)), scalars, image, acc, bias)
    out = share(out).reshape(GROUP, rows, side, split)
    return jnp.moveaxis(out, 0, 2).reshape(rows, side, out_local)


def solution(mesh):
    placed = (P("img", None, "ch"), P(None, None, "img", "ch"), P("ch"))
    return jax.shard_map(
        local, mesh=mesh, in_specs=placed, out_specs=P("img", None, "ch"), check_vma=False
    )
```
